256 devices in a mesh: ia: 8 (over z), ja: 4 (over x_hi, core), ka: 8 (over y, x_lo).
Axes of the slice: x: 4 (x_hi: 2, x_lo: 2; x = x_hi * 2 + x_lo), y: 4, z: 8, core: 2. Of those that a mesh axis runs over, the one named last changes fastest.
Arguments:
- tensor: bfloat16 [256, 512, 512], P('ka', 'ia', 'ja'), may hold values from -768 to 768
- observed: int32 [256, 512, 512], P('ka', 'ia', 'ja'), may hold values from 0 to 1, as said below
- factor_a: bfloat16 [512, 128], P('ia', ('ja', 'ka')), may hold values from -6 to 6
- factor_b: bfloat16 [512, 128], P('ja', ('ia', 'ka')), may hold values from -6 to 6
- factor_c: bfloat16 [256, 128], P('ka', ('ia', 'ja')), may hold values from -6 to 6
Outputs:
- step_a: float32 [512, 128], P('ia', ('ja', 'ka'))
- step_b: float32 [512, 128], P('ja', ('ia', 'ka'))
- step_c: float32 [256, 128], P('ka', ('ia', 'ja'))
The draws below stay inside these ranges and needn't reach their ends.
Inputs may be any that keep to these rules, and one draw needn't show every extreme that they name: `observed`: a 0/1 weight per cell.
All inputs are finite; a program needn't handle non-finite values.
Results may differ from the reference program's by a relative error of at most 0.0095.
Values may be sent and summed in bfloat16 or wider, within the bound.
No kernel may reach another device: no remote copies, remote signals or barrier semaphores. Data moves between devices by JAX's collectives and lax.ppermute only.
A program may use at most 64 MiB of HBM per device.

```python
import math
import jax
import jax.numpy as jnp
from jax import lax

RANK = 128
ITERS = 2
DIM_I = 512
DIM_J = 512
DIM_K = 256


def draw_observed(key, part):
    level_key = jax.random.fold_in(key, 11)
    cell_key = jax.random.fold_in(key, 23)
    blocks_k = (DIM_K + 3) // 4
    blocks_i = (DIM_I + 7) // 8
    blocks_j = (DIM_J + 31) // 32
    levels = jax.random.randint(level_key, (blocks_k, blocks_i, blocks_j), 0, 8)
    per_mille = jnp.array([10, 14, 19, 27, 37, 52, 72, 100], jnp.int32)
    limits = jnp.take(per_mille, levels)
    limits = jnp.broadcast_to(limits[:, None, :, None, :, None], (blocks_k, 4, blocks_i, 8, blocks_j, 32))
    limits = limits.reshape(blocks_k * 4, blocks_i * 8, blocks_j * 32)[:DIM_K, :DIM_I, :DIM_J]
    position = jnp.arange(DIM_I, dtype=jnp.int32)
    rising = (DIM_I + 9 * position)[None, :, None]
    limits = limits * rising // DIM_I
    chances = jax.random.randint(cell_key, (DIM_K, DIM_I, DIM_J), 0, 1000)
    return jnp.where(chances < limits, 1, 0).astype(jnp.int32)


def shard_levels(stream_key, extent, cuts, least, high):
    def one(dim, blocks):
        steps = jax.random.uniform(jax.random.fold_in(jax.random.fold_in(stream_key, 6), dim), (blocks,), jnp.float32, least / len(cuts), high / len(cuts))
        return jnp.repeat(jnp.exp(steps), extent[dim] // blocks).reshape((-1,) + (1,) * (len(extent) - dim - 1))

    gain = one(*cuts[0])
    for cut in cuts[1:]:
        gain = gain * one(*cut)
    return gain


def scatter_about(own_key, shape, scale, bound, pieces=(), held_as=jnp.bfloat16):
    entries = scale * jax.random.normal(own_key, shape, jnp.float32)
    if pieces:
        entries = entries * shard_levels(own_key, shape, pieces, -0.22, 0.18)
    return jnp.clip(entries, -bound, bound).astype(held_as)


def setup_inputs(seed: int = 0) -> dict:
    splits = jax.random.split(jax.random.key(seed), 6)
    tensor = scatter_about(splits[0], (DIM_K, DIM_I, DIM_J), 128.0, 768.0, ((0, 8), (1, 8), (2, 4)))
    observed = draw_observed(jax.random.fold_in(splits[5], 71), 0)
    factor_a = scatter_about(splits[2], (DIM_I, RANK), 1.0, 6.0, ((0, 8), (1, 32)))
    factor_b = scatter_about(splits[3], (DIM_J, RANK), 1.0, 6.0, ((0, 4), (1, 64)))
    factor_c = scatter_about(splits[4], (DIM_K, RANK), 1.0, 6.0, ((0, 8), (1, 32)))
    return {"tensor": tensor, "observed": observed, "factor_a": factor_a, "factor_b": factor_b, "factor_c": factor_c}


DAMP = 1.0


def against(left_side, right_side):
    return lax.dot_general(left_side, right_side, (((1,), (1,)), ((), ())), preferred_element_type=jnp.float32)


def reference(tensor, observed, factor_a, factor_b, factor_c):
    divisor = DIM_J * DIM_K / 32.0
    blocked = math.gcd(DIM_K, 8)
    count_blocks = DIM_K // blocked
    slabs = tensor.reshape(count_blocks, blocked, DIM_I, DIM_J)
    holes_all = observed.reshape(count_blocks, blocked, DIM_I, DIM_J)
    c_blocks = factor_c.reshape(count_blocks, blocked, RANK)
    wide_a = factor_a.astype(jnp.float32)

    def sweep(builder, extra):
        def advance(carry, inputs):
            slab, holes, c_block, hat_block = inputs
            wide_block = c_block.astype(jnp.float32)
            paired = (wide_block[:, None, :] * wide_a[None, :, :]).astype(jnp.bfloat16).reshape(blocked * DIM_I, RANK)
            weighted = builder(slab, holes, paired, wide_block, hat_block)
            part_b = lax.dot_general(weighted, paired, (((0,), (0,)), ((), ())), preferred_element_type=jnp.float32)
            mixture = jnp.dot(weighted, factor_b, preferred_element_type=jnp.float32).reshape(blocked, DIM_I, RANK)
            part_a = jnp.einsum("kir,kr->ir", mixture, wide_block)
            part_c = jnp.einsum("kir,ir->kr", mixture, wide_a)
            return (carry[0] + part_a, carry[1] + part_b), part_c

        start = (jnp.zeros((DIM_I, RANK), jnp.float32), jnp.zeros((DIM_J, RANK), jnp.float32))
        sums, parts_c = lax.scan(advance, start, (slabs, holes_all, c_blocks, extra))
        return sums[0], sums[1], parts_c.reshape(DIM_K, RANK)

    def residual_tile(slab, holes, paired, wide_block, hat_block):
        fitted = against(paired, factor_b)
        values = slab.reshape(-1, DIM_J).astype(jnp.float32)
        return (holes.reshape(-1, DIM_J).astype(jnp.float32) * (values - fitted) / divisor).astype(jnp.bfloat16)

    def hessian_times(direction):
        hat_a = direction[0].astype(jnp.bfloat16).astype(jnp.float32)
        hat_b = direction[1].astype(jnp.bfloat16)
        hat_c = direction[2].astype(jnp.bfloat16).reshape(count_blocks, blocked, RANK)

        def tangent_tile(slab, holes, paired, wide_block, hat_block):
            sideways = hat_block.astype(jnp.float32)[:, None, :] * wide_a[None, :, :] + wide_block[:, None, :] * hat_a[None, :, :]
            sideways = sideways.astype(jnp.bfloat16).reshape(blocked * DIM_I, RANK)
            tangent = against(paired, hat_b) + against(sideways, factor_b)
            return (holes.reshape(-1, DIM_J).astype(jnp.float32) * tangent / divisor).astype(jnp.bfloat16)

        parts = sweep(tangent_tile, hat_c)
        return tuple(part + DAMP * vector for part, vector in zip(parts, direction))

    def inner_sum(first, second):
        return sum(jnp.sum(left_side * right_side) for left_side, right_side in zip(first, second))

    gradient = sweep(residual_tile, c_blocks)
    solution = tuple(jnp.zeros_like(vector) for vector in gradient)
    residual = gradient
    direction = gradient
    norm_now = inner_sum(residual, residual)
    for iteration in range(ITERS):
        product = hessian_times(direction)
        step_size = norm_now / inner_sum(direction, product)
        solution = tuple(vector + step_size * update for vector, update in zip(solution, direction))
        if iteration + 1 < ITERS:
            residual = tuple(vector - step_size * update for vector, update in zip(residual, product))
            norm_next = inner_sum(residual, residual)
            direction = tuple(vector + (norm_next / norm_now) * update for vector, update in zip(residual, direction))
            norm_now = norm_next
    return solution[0], solution[1], solution[2]
```

```python
import jax
import jax.numpy as jnp
from jax import lax
from jax.sharding import Mesh
from jax.sharding import PartitionSpec as P

JA = ("ja_0", "ja_1")
KA = ("ka_0", "ka_1")
PLANE = ("ja_0", "ja_1", "ka_0", "ka_1")
IA_KA = ("ia", "ka_0", "ka_1")
IA_JA = ("ia", "ja_0", "ja_1")
EVERY = ("ia", "ja_0", "ja_1", "ka_0", "ka_1")
F32, BF16 = jnp.float32, jnp.bfloat16


def exchange(blocks, axes):
    return lax.all_to_all(blocks, axes, 0, 0, tiled=True)


def to_everyone(row, axes):
    count = lax.axis_size(axes)
    return exchange(jnp.broadcast_to(row[None], (count, *row.shape)), axes)


def local(tensor, observed, factor_a, factor_b, factor_c):
    depth, height, width = tensor.shape
    n_z, n_j, n_k = lax.axis_size("ia"), lax.axis_size(JA), lax.axis_size(KA)
    z, jb, kb = lax.axis_index("ia"), lax.axis_index(JA), lax.axis_index(KA)
    cols_a, cols_b, cols_c = factor_a.shape[1], factor_b.shape[1], factor_c.shape[1]
    plane = n_j * n_k
    rank = cols_a * plane
    divisor = width * n_j * (depth * n_k) / 32.0

    packed = jnp.concatenate([factor_a.T.ravel(), factor_b.T.ravel(), factor_c.T.ravel()])
    everything = to_everyone(packed[None], EVERY).reshape(n_z, n_j, n_k, -1)
    s_a, s_b = factor_a.size, factor_b.size
    at = lax.dynamic_index_in_dim(everything[..., :s_a], z, 0, False).reshape(rank, height)
    bt = lax.dynamic_index_in_dim(everything[..., s_a : s_a + s_b], jb, 1, False).reshape(rank, width)
    ct = lax.dynamic_index_in_dim(everything[..., s_a + s_b :], kb, 2, False).reshape(rank, depth)

    weight = observed.reshape(depth * height, width).astype(F32) * (1.0 / divisor)
    wide_a, wide_c = at.T.astype(F32), ct.T.astype(F32)
    paired = (wide_c[:, None, :] * wide_a[None]).astype(BF16).reshape(depth * height, rank)

    def reduced(weighted, scalars):
        part_b = lax.dot_general(paired, weighted, (((0,), (0,)), ((), ())), preferred_element_type=F32)
        mixture = lax.dot_general(weighted, bt, (((1,), (1,)), ((), ())), preferred_element_type=F32)
        mixture = mixture.reshape(depth, height, rank)
        part_a = jnp.sum(mixture * wide_c[:, None, :], axis=0).T
        part_c = jnp.sum(mixture * wide_a[None], axis=1).T
        extra = jnp.broadcast_to(scalars[None], (rank, scalars.size))
        payload = jnp.concatenate([part_b, part_a, part_c, extra], axis=1)
        got = exchange(payload.reshape(plane, cols_a, -1), PLANE)
        got = got.reshape(n_j, n_k, cols_a, -1)
        own_b = jnp.sum(got[..., :width], axis=1)
        rest = got[..., width:]
        own_a = jnp.sum(rest[..., :height], axis=(0, 1))
        own_c = jnp.sum(rest[..., height : height + depth], axis=0)
        own_s = jnp.sum(rest[..., height + depth :], axis=(0, 1))[0]
        line = jnp.concatenate([own_b.ravel(), own_c.ravel(), own_s])
        line = jnp.sum(to_everyone(line[None], "ia"), axis=0)[0]
        own_b = line[: own_b.size].reshape(own_b.shape)
        own_c = line[own_b.size : own_b.size + own_c.size].reshape(own_c.shape)
        totals = line[own_b.size + own_c.size :]
        back = jnp.concatenate(
            [
                jnp.broadcast_to(own_b[:, None], (n_j, n_k, cols_a, width)),
                jnp.broadcast_to(own_a[None, None], (n_j, n_k, cols_a, height)),
                jnp.broadcast_to(own_c[None], (n_j, n_k, cols_a, depth)),
            ],
            axis=-1,
        )
        full = exchange(back.reshape(plane, cols_a, -1), PLANE).reshape(rank, -1)
        return full, totals

    def split(full):
        return full[:, width : width + height], full[:, :width], full[:, width + height :]

    def shared(first, second):
        a, b, c = (jnp.sum(x) for x in split(first * second))
        return a / plane + b / (n_z * n_k) + c / (n_z * n_j)

    def tangent_of(full):
        hat_at, hat_bt, hat_ct = (x.astype(BF16) for x in split(full))
        hat_a, hat_c = hat_at.T.astype(F32), hat_ct.T.astype(F32)
        sideways = (hat_c[:, None, :] * wide_a[None] + wide_c[:, None, :] * hat_a[None]).astype(BF16)
        left = jnp.concatenate([paired, sideways.reshape(depth * height, rank)], axis=1)
        right = jnp.concatenate([hat_bt, bt], axis=0)
        return jnp.dot(left, right, preferred_element_type=F32)

    room = 32
    fitted = jnp.dot(paired, bt, preferred_element_type=F32)
    values = tensor.reshape(depth * height, width).astype(F32)
    errors = (weight * (values - fitted)).astype(BF16)
    gradient, _ = reduced(errors, jnp.zeros((room,), F32))

    tangent_g = tangent_of(gradient)
    weighted_g = weight * tangent_g
    mine = jnp.stack([shared(gradient, gradient), jnp.sum(weighted_g * tangent_g)])
    mine = jnp.pad(mine, (0, room - 2))
    product, totals = reduced(weighted_g.astype(BF16), mine)
    gg, gwg = totals[0], totals[1]
    alpha = gg / (gg + gwg)
    residual = gradient - alpha * (product + gradient)

    tangent_r = tangent_of(residual)
    weighted_r = weight * tangent_r
    mine = jnp.stack(
        [
            shared(residual, residual),
            shared(residual, gradient),
            jnp.sum(weighted_r * tangent_r),
            jnp.sum(weighted_r * tangent_g),
        ]
    )
    totals = jnp.sum(to_everyone(jnp.pad(mine, (0, 124))[None], EVERY), axis=0)[0]
    rr, rg, rwr, rwg = totals[0], totals[1], totals[2], totals[3]
    beta = rr / gg
    curve = (rwr + rr) + 2.0 * beta * (rwg + rg) + beta * beta * (gwg + gg)
    step = rr / curve
    result_a, result_b, result_c = split((alpha + step * beta) * gradient + step * residual)
    step_a = lax.dynamic_slice_in_dim(result_a, (jb * n_k + kb) * cols_a, cols_a, 0).T
    step_b = lax.dynamic_slice_in_dim(result_b, (z * n_k + kb) * cols_b, cols_b, 0).T
    step_c = lax.dynamic_slice_in_dim(result_c, (z * n_j + jb) * cols_c, cols_c, 0).T
    return step_a, step_b, step_c


def solution(mesh):
    torus = Mesh(mesh.devices.reshape(mesh.shape["ia"], 2, 2, 4, 2), EVERY)
    return jax.shard_map(
        local,
        mesh=torus,
        in_specs=(P(KA, "ia", JA), P(KA, "ia", JA), P("ia", PLANE), P(JA, IA_KA), P(KA, IA_JA)),
        out_specs=(P("ia", PLANE), P(JA, IA_KA), P(KA, IA_JA)),
        check_vma=False,
    )
```

```python
import jax
import jax.numpy as jnp
from jax import lax
from jax.experimental import pallas as pl
from jax.experimental.pallas import tpu as pltpu
from jax.sharding import Mesh
from jax.sharding import PartitionSpec as P

JA = ("ja_0", "ja_1")
KA = ("ka_0", "ka_1")
PLANE = ("ja_0", "ja_1", "ka_0", "ka_1")
IA_KA = ("ia", "ka_0", "ka_1")
IA_JA = ("ia", "ja_0", "ja_1")
EVERY = ("ia", "ja_0", "ja_1", "ka_0", "ka_1")
F32, BF16 = jnp.float32, jnp.bfloat16
DEPTH, HEIGHT, WIDTH, RANK = 32, 64, 128, 128
CELLS = DEPTH * HEIGHT
N_Z, N_J, N_K = 8, 4, 8
EACH = 4
ROWS = EACH * HEIGHT
SCALE = 1.0 / 4096.0
AB = HEIGHT + WIDTH
BC = WIDTH + DEPTH


def exchange(blocks, axes):
    return lax.all_to_all(blocks, axes, 0, 0, tiled=True)


def across_ja(x):
    return [x] + [lax.ppermute(x, JA, [(i, i ^ m) for i in range(N_J)]) for m in (1, 2, 3)]


def call(kernel, outs, *operands, scratch=()):
    return pl.pallas_call(
        kernel,
        out_shape=[jax.ShapeDtypeStruct(shape, dtype) for shape, dtype in outs],
        in_specs=[
            pl.BlockSpec(memory_space=pltpu.SMEM if x.dtype == jnp.int32 and x.ndim == 1 else pltpu.VMEM)
            for x in operands
        ],
        out_specs=[pl.BlockSpec(memory_space=pltpu.VMEM) for _ in outs],
        scratch_shapes=[pltpu.VMEM(shape, dtype) for shape, dtype in scratch],
        compiler_params=pltpu.CompilerParams(vmem_limit_bytes=48 * 2**20),
    )(*operands)


def pack_kernel(a_ref, b_ref, c_ref, sent_ref, own_ref, wide):
    wide[...] = jnp.zeros_like(wide)
    wide[0:HEIGHT, 0:4] = a_ref[...].astype(F32)
    wide[HEIGHT : HEIGHT + DEPTH, 0:4] = c_ref[...].astype(F32)
    wide[128:256, 0:2] = b_ref[...].astype(F32)
    a_and_c = wide[0:128, :].T[0:4]
    b = wide[128:256, :].T[0:2]
    own_ref[0:4, :] = a_and_c
    own_ref[4:6, :] = b
    own_ref[6:8, :] = jnp.zeros((2, 128), F32)
    for peer in range(N_K):
        sent_ref[peer] = own_ref[...]


def repack_kernel(got_ref, c0, c1, c2, c3, sent_ref, a_ref, rows_a, rows_b, rows_c):
    for peer in range(N_K):
        rows_a[4 * peer : 4 * peer + 4, :] = got_ref[peer, 0:4, :]
        rows_b[2 * peer : 2 * peer + 2, :] = got_ref[peer, 4:6, :]
    for m, piece in enumerate((c0, c1, c2, c3)):
        rows_c[4 * m : 4 * m + 4, :] = piece[0:4, :]
    a_ref[...] = rows_a[...].astype(BF16)
    b, c = rows_b[...].astype(BF16), rows_c[...].astype(BF16)
    for peer in range(N_Z):
        sent_ref[peer, 0:16, :] = b
        sent_ref[peer, 16:32, :] = c


def xor_lanes(x, bit, on):
    lane = lax.broadcasted_iota(jnp.int32, x.shape, 1)
    swapped = jnp.where((lane & bit) != 0, pltpu.roll(x, bit, 1), pltpu.roll(x, 128 - bit, 1))
    return jnp.where(on != 0, swapped, x)


def in_pairs(k, a, c_ref):
    return jnp.concatenate([c_ref[pl.ds(k + s, 1), :] * a for s in range(EACH)], axis=0)


def weight_of(seen_ref, k):
    seen = seen_ref[pl.ds(k, EACH), :, :].reshape(ROWS, WIDTH)
    return seen.astype(F32) * SCALE


def add_products(k, weighted, paired, a, b, c_ref, part_a, part_b, part_c):
    part_b[...] += lax.dot_general(weighted, paired, (((0,), (0,)), ((), ())), preferred_element_type=F32)
    mixture = jnp.dot(weighted, b, preferred_element_type=F32)
    total = part_a[...]
    for s in range(EACH):
        slab = mixture[s * HEIGHT : (s + 1) * HEIGHT]
        total = total + slab * c_ref[pl.ds(k + s, 1), :]
        part_c[pl.ds(k + s, 1), :] = jnp.sum(slab * a, axis=0, keepdims=True)
    part_a[...] = total


def hand_out(part_a, part_b, part_c, sent_ref, c_out):
    a, b = part_a[...].astype(BF16), part_b[...].astype(BF16)
    for peer in range(N_K):
        sent_ref[peer, 0:HEIGHT, :] = a
        sent_ref[peer, HEIGHT:AB, :] = b
    c_out[...] = part_c[...].astype(BF16)


def first_kernel(place, got_ref, a0, a1, a2, a3, values_ref, seen_ref,
                 sent_ref, c_out, fa_ref, fb_ref, fbt_ref, fc_ref, part_a, part_b, part_c):
    a = jnp.concatenate([x[...].astype(F32) for x in (a0, a1, a2, a3)], axis=0).T[0:HEIGHT]
    a = xor_lanes(xor_lanes(a, 32, place[0] & 1), 64, place[0] & 2)
    c = jnp.concatenate([got_ref[z, 16:32, :].astype(F32) for z in range(N_Z)], axis=0).T[HEIGHT : HEIGHT + DEPTH]
    c = xor_lanes(xor_lanes(c, 4, place[0] & 1), 8, place[0] & 2)
    bt = jnp.concatenate([got_ref[z, 0:16, :].astype(F32) for z in range(N_Z)], axis=0)
    fbt_ref[...] = bt.astype(BF16)
    fb_ref[...] = bt.T.astype(BF16)
    fa_ref[...] = a
    fc_ref[...] = c
    part_a[...] = jnp.zeros_like(part_a)
    part_b[...] = jnp.zeros_like(part_b)

    @pl.loop(0, DEPTH, step=EACH)
    def _(k):
        a = fa_ref[...]
        paired = in_pairs(k, a, fc_ref).astype(BF16)
        fitted = jnp.dot(paired, fbt_ref[...], preferred_element_type=F32)
        values = values_ref[pl.ds(k, EACH), :, :].reshape(ROWS, WIDTH).astype(F32)
        errors = (weight_of(seen_ref, k) * (values - fitted)).astype(BF16)
        add_products(k, errors, paired, a, fb_ref[...], fc_ref, part_a, part_b, part_c)

    hand_out(part_a, part_b, part_c, sent_ref, c_out)


def middle_kernel(got_ref, c0, c1, c2, c3, sent_ref, a_ref):
    total = got_ref[0].astype(F32)
    for peer in range(1, N_K):
        total = total + got_ref[peer].astype(F32)
    a_ref[...] = total[0:HEIGHT].astype(BF16)
    b = total[HEIGHT:AB].astype(BF16)
    c = ((c0[...].astype(F32) + c1[...].astype(F32)) + (c2[...].astype(F32) + c3[...].astype(F32))).astype(BF16)
    for peer in range(N_Z):
        sent_ref[peer, 0:WIDTH, :] = b
        sent_ref[peer, WIDTH:BC, :] = c


def take_totals(got_ref, a0, a1, a2, a3, out):
    total = got_ref[0].astype(F32)
    for peer in range(1, N_Z):
        total = total + got_ref[peer].astype(F32)
    out[0:HEIGHT, :] = (a0[...].astype(F32) + a1[...].astype(F32)) + (a2[...].astype(F32) + a3[...].astype(F32))
    out[HEIGHT : HEIGHT + BC, :] = total


def tangent_at(k, paired, fa_ref, fc_ref, fbt_ref, hat_a, hat_bt, hat_c):
    sideways = (in_pairs(k, fa_ref[...], hat_c) + in_pairs(k, hat_a[...], fc_ref)).astype(BF16)
    return jnp.dot(paired, hat_bt[...], preferred_element_type=F32) + jnp.dot(
        sideways, fbt_ref[...], preferred_element_type=F32
    )


def round_hats(direction, hat_a, hat_bt, hat_c):
    hat_a[...] = direction[0:HEIGHT].astype(BF16).astype(F32)
    hat_bt[...] = direction[HEIGHT:AB].T.astype(BF16)
    hat_c[...] = direction[AB:].astype(BF16).astype(F32)


def second_kernel(got_ref, a0, a1, a2, a3, seen_ref, fa_ref, fb_ref, fbt_ref, fc_ref,
                  sent_ref, c_out, grad_ref, tangent_ref, sum_ref,
                  part_a, part_b, part_c, hat_a, hat_bt, hat_c):
    take_totals(got_ref, a0, a1, a2, a3, grad_ref)
    round_hats(grad_ref[...], hat_a, hat_bt, hat_c)
    part_a[...] = jnp.zeros_like(part_a)
    part_b[...] = jnp.zeros_like(part_b)
    sum_ref[...] = jnp.zeros_like(sum_ref)

    @pl.loop(0, DEPTH, step=EACH)
    def _(k):
        a = fa_ref[...]
        paired = in_pairs(k, a, fc_ref).astype(BF16)
        tangent = tangent_at(k, paired, fa_ref, fc_ref, fbt_ref, hat_a, hat_bt, hat_c)
        weighted = weight_of(seen_ref, k) * tangent
        tangent_ref[pl.ds(k * HEIGHT, ROWS), :] = tangent
        sum_ref[...] += jnp.sum((weighted * tangent).reshape(ROWS // 8, 8, WIDTH), axis=0)
        add_products(k, weighted.astype(BF16), paired, a, fb_ref[...], fc_ref, part_a, part_b, part_c)

    hand_out(part_a, part_b, part_c, sent_ref, c_out)


def total_of(x):
    return jnp.sum(jnp.sum(x, axis=0, keepdims=True), axis=1, keepdims=True)


def share_of(x):
    return (
        total_of(x[0:HEIGHT]) * (1.0 / (N_J * N_K))
        + total_of(x[HEIGHT:AB]) * (1.0 / (N_Z * N_K))
        + total_of(x[AB:]) * (1.0 / (N_Z * N_J))
    )


def third_kernel(got_ref, a0, a1, a2, a3, seen_ref, fa_ref, fbt_ref, fc_ref, grad_ref, tangent_ref, sum_ref,
                 sent_ref, rest_ref, hat_a, hat_bt, hat_c, sum_rest, sum_both):
    take_totals(got_ref, a0, a1, a2, a3, rest_ref)
    grad, product = grad_ref[...], rest_ref[...]
    length = share_of(grad * grad)
    level = jnp.where(length > 0.0, share_of(grad * product) / jnp.where(length > 0.0, length, 1.0), 0.0)
    rest = product - level * grad
    rest_ref[...] = rest
    round_hats(rest, hat_a, hat_bt, hat_c)
    sum_rest[...] = jnp.zeros_like(sum_rest)
    sum_both[...] = jnp.zeros_like(sum_both)

    @pl.loop(0, DEPTH, step=EACH)
    def _(k):
        paired = in_pairs(k, fa_ref[...], fc_ref).astype(BF16)
        tangent = tangent_at(k, paired, fa_ref, fc_ref, fbt_ref, hat_a, hat_bt, hat_c)
        weighted = weight_of(seen_ref, k) * tangent
        before = tangent_ref[pl.ds(k * HEIGHT, ROWS), :]
        sum_rest[...] += jnp.sum((weighted * tangent).reshape(ROWS // 8, 8, WIDTH), axis=0)
        sum_both[...] += jnp.sum((weighted * before).reshape(ROWS // 8, 8, WIDTH), axis=0)

    lane = lax.broadcasted_iota(jnp.int32, (1, 128), 1)
    line = jnp.zeros((1, 128), F32)
    for place, value in enumerate(
        (
            level,
            length,
            share_of(grad * rest),
            share_of(rest * rest),
            total_of(sum_ref[...]),
            total_of(sum_both[...]),
            total_of(sum_rest[...]),
        )
    ):
        line = jnp.where(lane == place, value, line)
    for peer in range(N_Z * N_J * N_K):
        sent_ref[peer] = line


def last_kernel(place, got_ref, own_ref, grad_ref, rest_ref, a_ref, b_ref, c_ref):
    table = got_ref[:, 0, :].T
    level, gg, gv, vv, s_gg, s_gv, s_vv = (table[i : i + 1] for i in range(7))

    def add(x):
        return jnp.sum(x, axis=1, keepdims=True)

    norm = add(gg)
    alpha = norm / (norm + add(s_gg))
    near = 1.0 - alpha * (1.0 + level)
    rr = add(near * near * gg - 2.0 * alpha * near * gv + alpha * alpha * vv)
    rg = add(near * gg - alpha * gv)
    s_rr = add(near * near * s_gg - 2.0 * alpha * near * s_gv + alpha * alpha * s_vv)
    s_rg = add(near * s_gg - alpha * s_gv)
    beta = rr / norm
    curve = (s_rr + rr) + 2.0 * beta * (s_rg + rg) + beta * beta * (add(s_gg) + norm)
    step = rr / curve
    own_level = own_ref[0, :, 0:1]
    own_near = 1.0 - alpha * (1.0 + own_level)
    x = (alpha + step * (own_near + beta)) * grad_ref[...] - (step * alpha) * rest_ref[...]
    z, jb, kb = place[1], place[0], place[2]
    a_ref[...] = pltpu.roll(x[0:HEIGHT], (128 - (jb * N_K + kb) * 4) % 128, 1)[:, 0:4]
    b_ref[...] = pltpu.roll(x[HEIGHT:AB], (128 - (z * N_K + kb) * 2) % 128, 1)[:, 0:2]
    c_ref[...] = pltpu.roll(x[AB:], (128 - (z * N_J + jb) * 4) % 128, 1)[:, 0:4]


def local(tensor, observed, factor_a, factor_b, factor_c):
    z, jb, kb = lax.axis_index("ia"), lax.axis_index(JA), lax.axis_index(KA)
    place = jnp.stack([jb, z, kb]).astype(jnp.int32)
    tile = lambda rows: ((rows, RANK), F32)
    sums = [tile(HEIGHT), tile(WIDTH), tile(DEPTH)]
    hats = [tile(HEIGHT), ((RANK, WIDTH), BF16), tile(DEPTH)]

    sent, own = call(
        pack_kernel, [((N_K, 8, 128), F32), ((8, 128), F32)], factor_a, factor_b, factor_c, scratch=[tile(256)]
    )
    got = exchange(sent, KA)
    sent, own = call(
        repack_kernel, [((N_Z, 32, 128), BF16), ((32, 128), BF16)], got, *across_ja(own),
        scratch=[tile(32), tile(16), tile(16)],
    )
    got = exchange(sent, "ia")

    sent_types = [((N_K, AB, RANK), BF16), ((DEPTH, RANK), BF16)]
    sent, part_c, fa, fb, fbt, fc = call(
        first_kernel,
        sent_types + [tile(HEIGHT), ((WIDTH, RANK), BF16), ((RANK, WIDTH), BF16), tile(DEPTH)],
        place, got, *across_ja(own), tensor, observed, scratch=sums,
    )

    def summed(sent, part_c):
        got = exchange(sent, KA)
        sent, part_a = call(
            middle_kernel, [((N_Z, BC, RANK), BF16), ((HEIGHT, RANK), BF16)], got, *across_ja(part_c)
        )
        return exchange(sent, "ia"), *across_ja(part_a)

    sent, part_c, grad, tangent, sum_gg = call(
        second_kernel,
        sent_types + [tile(AB + DEPTH), tile(CELLS), tile(8)],
        *summed(sent, part_c), observed, fa, fb, fbt, fc, scratch=sums + hats,
    )
    sent, rest = call(
        third_kernel,
        [((N_Z * N_J * N_K, 1, 128), F32), tile(AB + DEPTH)],
        *summed(sent, part_c), observed, fa, fbt, fc, grad, tangent, sum_gg, scratch=hats + [tile(8), tile(8)],
    )
    got = exchange(sent, EVERY)
    return tuple(
        call(
            last_kernel,
            [((HEIGHT, 4), F32), ((WIDTH, 2), F32), ((DEPTH, 4), F32)],
            place, got, sent[0:1], grad, rest,
        )
    )


def solution(mesh):
    torus = Mesh(mesh.devices.reshape(N_Z, 2, 2, 4, 2), EVERY)
    return jax.shard_map(
        local,
        mesh=torus,
        in_specs=(P(KA, "ia", JA), P(KA, "ia", JA), P("ia", PLANE), P(JA, IA_KA), P(KA, IA_JA)),
        out_specs=(P("ia", PLANE), P(JA, IA_KA), P(KA, IA_JA)),
        check_vma=False,
    )
```

```python
import jax
import jax.numpy as jnp
from jax import lax
from jax.experimental import pallas as pl
from jax.experimental.pallas import tpu as pltpu
from jax.sharding import Mesh
from jax.sharding import PartitionSpec as P

JA = ("ja_0", "ja_1")
KA = ("ka_0", "ka_1")
PLANE = ("ja_0", "ja_1", "ka_0", "ka_1")
IA_KA = ("ia", "ka_0", "ka_1")
IA_JA = ("ia", "ja_0", "ja_1")
EVERY = ("ia", "ja_0", "ja_1", "ka_0", "ka_1")
F32, BF16 = jnp.float32, jnp.bfloat16
DEPTH, HEIGHT, WIDTH, RANK = 32, 64, 128, 128
CELLS = DEPTH * HEIGHT
N_Z, N_J, N_K = 8, 4, 8
EACH = 8
ROWS = EACH * HEIGHT
SCALE = 1.0 / 4096.0
AB = HEIGHT + WIDTH
BC = WIDTH + DEPTH


def exchange(blocks, axes):
    return lax.all_to_all(blocks, axes, 0, 0, tiled=True)


def across_ja(x):
    return [x] + [lax.ppermute(x, JA, [(i, i ^ m) for i in range(N_J)]) for m in (1, 2, 3)]


def call(kernel, outs, *operands, scratch=()):
    return pl.pallas_call(
        kernel,
        out_shape=[jax.ShapeDtypeStruct(shape, dtype) for shape, dtype in outs],
        in_specs=[
            pl.BlockSpec(memory_space=pltpu.SMEM if x.dtype == jnp.int32 and x.ndim == 1 else pltpu.VMEM)
            for x in operands
        ],
        out_specs=[pl.BlockSpec(memory_space=pltpu.VMEM) for _ in outs],
        scratch_shapes=[pltpu.VMEM(shape, dtype) for shape, dtype in scratch],
        compiler_params=pltpu.CompilerParams(vmem_limit_bytes=48 * 2**20),
    )(*operands)


def pack_kernel(at_ref, bt_ref, ct_ref, sent_ref, own_ref):
    own_ref[...] = jnp.zeros_like(own_ref)
    own_ref[0:4, 0:HEIGHT] = at_ref[...].astype(F32)
    own_ref[0:4, HEIGHT : HEIGHT + DEPTH] = ct_ref[...].astype(F32)
    own_ref[4:6, :] = bt_ref[...].astype(F32)
    for peer in range(N_K):
        sent_ref[peer] = own_ref[...]


def repack_kernel(got_ref, c0, c1, c2, c3, sent_ref, a_ref, rows_a, rows_b, rows_c):
    for peer in range(N_K):
        rows_a[4 * peer : 4 * peer + 4, :] = got_ref[peer, 0:4, :]
        rows_b[2 * peer : 2 * peer + 2, :] = got_ref[peer, 4:6, :]
    for m, piece in enumerate((c0, c1, c2, c3)):
        rows_c[4 * m : 4 * m + 4, :] = piece[0:4, :]
    a_ref[...] = rows_a[...].astype(BF16)
    b, c = rows_b[...].astype(BF16), rows_c[...].astype(BF16)
    for peer in range(N_Z):
        sent_ref[peer, 0:16, :] = b
        sent_ref[peer, 16:32, :] = c


def xor_lanes(x, bit, on):
    lane = lax.broadcasted_iota(jnp.int32, x.shape, 1)
    swapped = jnp.where((lane & bit) != 0, pltpu.roll(x, bit, 1), pltpu.roll(x, 128 - bit, 1))
    return jnp.where(on != 0, swapped, x)


def in_pairs(k, a, c_ref):
    return jnp.concatenate([c_ref[pl.ds(k + s, 1), :] * a for s in range(EACH)], axis=0)


def weight_of(seen_ref, k):
    return seen_ref[pl.ds(k * HEIGHT, ROWS), :].astype(F32)


def add_products(k, weighted, paired, a, b, c_ref, part_a, part_b, part_c):
    part_b[...] += lax.dot_general(weighted, paired, (((0,), (0,)), ((), ())), preferred_element_type=F32)
    mixture = jnp.dot(weighted, b, preferred_element_type=F32)
    total = part_a[...]
    for s in range(EACH):
        slab = mixture[s * HEIGHT : (s + 1) * HEIGHT]
        total = total + slab * c_ref[pl.ds(k + s, 1), :]
        part_c[pl.ds(k + s, 1), :] = jnp.sum(slab * a, axis=0, keepdims=True)
    part_a[...] = total


def hand_out(part_a, part_b, part_c, sent_ref, c_out):
    a, b = part_a[...].astype(BF16), part_b[...].astype(BF16)
    for peer in range(N_K):
        sent_ref[peer, 0:HEIGHT, :] = a
        sent_ref[peer, HEIGHT:AB, :] = b
    c_out[...] = part_c[...].astype(BF16)


def first_kernel(place, got_ref, a0, a1, a2, a3, values_ref, seen_ref,
                 sent_ref, c_out, fa_ref, fb_ref, fbt_ref, fc_ref, part_a, part_b, part_c):
    a = jnp.concatenate([x[...].astype(F32) for x in (a0, a1, a2, a3)], axis=0).T[0:HEIGHT]
    a = xor_lanes(xor_lanes(a, 32, place[0] & 1), 64, place[0] & 2)
    c = jnp.concatenate([got_ref[z, 16:32, :].astype(F32) for z in range(N_Z)], axis=0).T[HEIGHT : HEIGHT + DEPTH]
    c = xor_lanes(xor_lanes(c, 4, place[0] & 1), 8, place[0] & 2)
    bt = jnp.concatenate([got_ref[z, 0:16, :].astype(F32) for z in range(N_Z)], axis=0)
    fbt_ref[...] = bt.astype(BF16)
    fb_ref[...] = bt.T.astype(BF16)
    fa_ref[...] = a
    fc_ref[...] = c
    part_a[...] = jnp.zeros_like(part_a)
    part_b[...] = jnp.zeros_like(part_b)

    @pl.loop(0, DEPTH, step=EACH, unroll=True)
    def _(k):
        a = fa_ref[...]
        paired = in_pairs(k, a, fc_ref).astype(BF16)
        fitted = jnp.dot(paired, fbt_ref[...], preferred_element_type=F32)
        values = values_ref[pl.ds(k * HEIGHT, ROWS), :].astype(F32)
        errors = (values - weight_of(seen_ref, k) * fitted).astype(BF16)
        add_products(k, errors, paired, a, fb_ref[...], fc_ref, part_a, part_b, part_c)

    hand_out(part_a, part_b, part_c, sent_ref, c_out)


def middle_kernel(got_ref, c0, c1, c2, c3, sent_ref, a_ref):
    total = got_ref[0].astype(F32)
    for peer in range(1, N_K):
        total = total + got_ref[peer].astype(F32)
    a_ref[...] = total[0:HEIGHT].astype(BF16)
    b = total[HEIGHT:AB].astype(BF16)
    c = ((c0[...].astype(F32) + c1[...].astype(F32)) + (c2[...].astype(F32) + c3[...].astype(F32))).astype(BF16)
    for peer in range(N_Z):
        sent_ref[peer, 0:WIDTH, :] = b
        sent_ref[peer, WIDTH:BC, :] = c


def take_totals(got_ref, a0, a1, a2, a3, out):
    total = got_ref[0].astype(F32)
    for peer in range(1, N_Z):
        total = total + got_ref[peer].astype(F32)
    out[0:HEIGHT, :] = (a0[...].astype(F32) + a1[...].astype(F32)) + (a2[...].astype(F32) + a3[...].astype(F32))
    out[HEIGHT : HEIGHT + BC, :] = total


def tangent_at(k, paired, fa_ref, fc_ref, fbt_ref, hat_a, hat_bt, hat_c):
    sideways = (in_pairs(k, fa_ref[...], hat_c) + in_pairs(k, hat_a[...], fc_ref)).astype(BF16)
    return jnp.dot(paired, hat_bt[...], preferred_element_type=F32) + jnp.dot(
        sideways, fbt_ref[...], preferred_element_type=F32
    )


def round_hats(direction, hat_a, hat_bt, hat_c):
    hat_a[...] = direction[0:HEIGHT].astype(BF16).astype(F32)
    hat_bt[...] = direction[HEIGHT:AB].T.astype(BF16)
    hat_c[...] = direction[AB:].astype(BF16).astype(F32)


def second_kernel(got_ref, a0, a1, a2, a3, seen_ref, fa_ref, fb_ref, fbt_ref, fc_ref,
                  sent_ref, c_out, grad_ref, tangent_ref, sum_ref,
                  part_a, part_b, part_c, hat_a, hat_bt, hat_c):
    take_totals(got_ref, a0, a1, a2, a3, grad_ref)
    round_hats(grad_ref[...], hat_a, hat_bt, hat_c)
    part_a[...] = jnp.zeros_like(part_a)
    part_b[...] = jnp.zeros_like(part_b)
    sum_ref[...] = jnp.zeros_like(sum_ref)

    @pl.loop(0, DEPTH, step=EACH, unroll=True)
    def _(k):
        a = fa_ref[...]
        paired = in_pairs(k, a, fc_ref).astype(BF16)
        tangent = tangent_at(k, paired, fa_ref, fc_ref, fbt_ref, hat_a, hat_bt, hat_c)
        weighted = weight_of(seen_ref, k) * tangent
        tangent_ref[pl.ds(k * HEIGHT, ROWS), :] = tangent
        sum_ref[...] += jnp.sum((weighted * tangent).reshape(ROWS // 8, 8, WIDTH), axis=0)
        add_products(k, weighted.astype(BF16), paired, a, fb_ref[...], fc_ref, part_a, part_b, part_c)

    hand_out(part_a, part_b, part_c, sent_ref, c_out)


def total_of(x):
    return jnp.sum(jnp.sum(x, axis=0, keepdims=True), axis=1, keepdims=True)


def share_of(x):
    return (
        total_of(x[0:HEIGHT]) * (1.0 / (N_J * N_K))
        + total_of(x[HEIGHT:AB]) * (1.0 / (N_Z * N_K))
        + total_of(x[AB:]) * (1.0 / (N_Z * N_J))
    )


def third_kernel(got_ref, a0, a1, a2, a3, seen_ref, fa_ref, fbt_ref, fc_ref, grad_ref, tangent_ref, sum_ref,
                 sent_ref, own_ref, rest_ref, hat_a, hat_bt, hat_c, sum_rest, sum_both):
    take_totals(got_ref, a0, a1, a2, a3, rest_ref)
    grad, product = grad_ref[...], rest_ref[...]
    length = share_of(grad * grad)
    level = jnp.where(length > 0.0, share_of(grad * product) / jnp.where(length > 0.0, length, 1.0), 0.0)
    rest = product - level * grad
    rest_ref[...] = rest
    round_hats(rest, hat_a, hat_bt, hat_c)
    sum_rest[...] = jnp.zeros_like(sum_rest)
    sum_both[...] = jnp.zeros_like(sum_both)

    @pl.loop(0, DEPTH, step=EACH, unroll=True)
    def _(k):
        paired = in_pairs(k, fa_ref[...], fc_ref).astype(BF16)
        tangent = tangent_at(k, paired, fa_ref, fc_ref, fbt_ref, hat_a, hat_bt, hat_c)
        weighted = weight_of(seen_ref, k) * tangent
        before = tangent_ref[pl.ds(k * HEIGHT, ROWS), :]
        sum_rest[...] += jnp.sum((weighted * tangent).reshape(ROWS // 8, 8, WIDTH), axis=0)
        sum_both[...] += jnp.sum((weighted * before).reshape(ROWS // 8, 8, WIDTH), axis=0)

    lane = lax.broadcasted_iota(jnp.int32, (1, 128), 1)
    line = jnp.zeros((1, 128), F32)
    for place, value in enumerate(
        (
            level,
            length,
            share_of(grad * rest),
            share_of(rest * rest),
            total_of(sum_ref[...]),
            total_of(sum_both[...]),
            total_of(sum_rest[...]),
        )
    ):
        line = jnp.where(lane == place, value, line)
    own_ref[...] = jnp.broadcast_to(line, (8, 128))
    for peer in range(N_Z * N_J * N_K):
        sent_ref[peer] = line


def columns_kernel(place, grad_ref, rest_ref, out_ref):
    z, jb, kb = place[1], place[0], place[2]
    for at, x in ((0, grad_ref), (16, rest_ref)):
        rows = pltpu.roll(x[0:HEIGHT, :], (128 - (jb * N_K + kb) * 4) % 128, 1).T
        out_ref[at : at + 4, 0:HEIGHT] = rows[0:4]
        rows = pltpu.roll(x[AB:, :], (128 - (z * N_J + jb) * 4) % 128, 1).T
        out_ref[at : at + 4, HEIGHT : HEIGHT + DEPTH] = rows[0:4]
        rows = pltpu.roll(x[HEIGHT:AB, :], (128 - (z * N_K + kb) * 2) % 128, 1).T
        out_ref[at + 8 : at + 10, :] = rows[0:2]


def last_kernel(got_ref, own_ref, columns_ref, a_ref, b_ref, c_ref):
    table = got_ref[:, 0, :].T
    level, gg, gv, vv, s_gg, s_gv, s_vv = (table[i : i + 1] for i in range(7))

    def add(x):
        return jnp.sum(x, axis=1, keepdims=True)

    norm, norm_seen = add(gg), add(s_gg)
    alpha = norm / (norm + norm_seen)
    near = 1.0 - alpha * (1.0 + level)
    rr = add(near * near * gg - 2.0 * alpha * near * gv + alpha * alpha * vv)
    rg = add(near * gg - alpha * gv)
    s_rr = add(near * near * s_gg - 2.0 * alpha * near * s_gv + alpha * alpha * s_vv)
    s_rg = add(near * s_gg - alpha * s_gv)
    beta = rr / norm
    curve = (s_rr + rr) + 2.0 * beta * (s_rg + rg) + beta * beta * (norm_seen + norm)
    step = rr / curve
    own_near = 1.0 - alpha * (1.0 + own_ref[0:1, 0:1])
    x = (alpha + step * (own_near + beta)) * columns_ref[0:16, :] - (step * alpha) * columns_ref[16:32, :]
    a_ref[...] = x[0:4, 0:HEIGHT]
    c_ref[...] = x[0:4, HEIGHT : HEIGHT + DEPTH]
    b_ref[...] = x[8:10, :]


def local(tensor, observed, factor_a, factor_b, factor_c):
    z, jb, kb = lax.axis_index("ia"), lax.axis_index(JA), lax.axis_index(KA)
    place = jnp.stack([jb, z, kb]).astype(jnp.int32)
    weight = (observed.astype(F32) * SCALE).astype(BF16).reshape(CELLS, WIDTH)
    values = tensor.reshape(CELLS, WIDTH) * weight
    tile = lambda rows: ((rows, RANK), F32)
    sums = [tile(HEIGHT), tile(WIDTH), tile(DEPTH)]
    hats = [tile(HEIGHT), ((RANK, WIDTH), BF16), tile(DEPTH)]

    sent, own = call(
        pack_kernel, [((N_K, 8, 128), F32), ((8, 128), F32)], factor_a.T, factor_b.T, factor_c.T
    )
    got = exchange(sent, KA)
    sent, own = call(
        repack_kernel, [((N_Z, 32, 128), BF16), ((32, 128), BF16)], got, *across_ja(own),
        scratch=[tile(32), tile(16), tile(16)],
    )
    got = exchange(sent, "ia")

    sent_types = [((N_K, AB, RANK), BF16), ((DEPTH, RANK), BF16)]
    sent, part_c, fa, fb, fbt, fc = call(
        first_kernel,
        sent_types + [tile(HEIGHT), ((WIDTH, RANK), BF16), ((RANK, WIDTH), BF16), tile(DEPTH)],
        place, got, *across_ja(own), values, weight, scratch=sums,
    )

    def summed(sent, part_c):
        got = exchange(sent, KA)
        sent, part_a = call(
            middle_kernel, [((N_Z, BC, RANK), BF16), ((HEIGHT, RANK), BF16)], got, *across_ja(part_c)
        )
        return exchange(sent, "ia"), *across_ja(part_a)

    sent, part_c, grad, tangent, sum_gg = call(
        second_kernel,
        sent_types + [tile(AB + DEPTH), tile(CELLS), tile(8)],
        *summed(sent, part_c), weight, fa, fb, fbt, fc, scratch=sums + hats,
    )
    sent, own, rest = call(
        third_kernel,
        [((N_Z * N_J * N_K, 1, 128), F32), tile(8), tile(AB + DEPTH)],
        *summed(sent, part_c), weight, fa, fbt, fc, grad, tangent, sum_gg, scratch=hats + [tile(8), tile(8)],
    )
    (columns,) = call(columns_kernel, [tile(32)], place, grad, rest)
    got = exchange(sent, EVERY)
    steps = call(last_kernel, [((4, HEIGHT), F32), ((2, WIDTH), F32), ((4, DEPTH), F32)], got, own, columns)
    return tuple(x.T for x in steps)


def solution(mesh):
    torus = Mesh(mesh.devices.reshape(N_Z, 2, 2, 4, 2), EVERY)
    return jax.shard_map(
        local,
        mesh=torus,
        in_specs=(P(KA, "ia", JA), P(KA, "ia", JA), P("ia", PLANE), P(JA, IA_KA), P(KA, IA_JA)),
        out_specs=(P("ia", PLANE), P(JA, IA_KA), P(KA, IA_JA)),
        check_vma=False,
    )
```

```python
import jax
import jax.numpy as jnp
from jax import lax
from jax.experimental import pallas as pl
from jax.experimental.pallas import tpu as pltpu
from jax.sharding import Mesh
from jax.sharding import PartitionSpec as P

JA = ("ja_0", "ja_1")
KA = ("ka_0", "ka_1")
PLANE = ("ja_0", "ja_1", "ka_0", "ka_1")
IA_KA = ("ia", "ka_0", "ka_1")
IA_JA = ("ia", "ja_0", "ja_1")
EVERY = ("ia", "ja_0", "ja_1", "ka_0", "ka_1")
F32, BF16 = jnp.float32, jnp.bfloat16
DEPTH, HEIGHT, WIDTH, RANK = 32, 64, 128, 128
CELLS = DEPTH * HEIGHT
N_Z, N_J, N_K = 8, 4, 8
EACH = 8
ROWS = EACH * HEIGHT
SCALE = 1.0 / 4096.0
AB = HEIGHT + WIDTH
BC = WIDTH + DEPTH


def exchange(blocks, axes):
    return lax.all_to_all(blocks, axes, 0, 0, tiled=True)


def swapped(x, axis):
    return lax.ppermute(x, axis, [(0, 1), (1, 0)])


def over_ja(x):
    x = x + swapped(x, "ja_1")
    return x + swapped(x, "ja_0")


def call(kernel, outs, *operands, scratch=()):
    return pl.pallas_call(
        kernel,
        out_shape=[jax.ShapeDtypeStruct(shape, dtype) for shape, dtype in outs],
        in_specs=[
            pl.BlockSpec(memory_space=pltpu.SMEM if x.dtype == jnp.int32 and x.ndim == 1 else pltpu.VMEM)
            for x in operands
        ],
        out_specs=[pl.BlockSpec(memory_space=pltpu.VMEM) for _ in outs],
        scratch_shapes=[pltpu.VMEM(shape, dtype) for shape, dtype in scratch],
        compiler_params=pltpu.CompilerParams(vmem_limit_bytes=48 * 2**20),
    )(*operands)


def pack_kernel(at_ref, bt_ref, ct_ref, sent_ref, block):
    block[...] = jnp.zeros_like(block)
    block[0:4, 0:HEIGHT] = at_ref[...].astype(F32)
    block[0:4, HEIGHT : HEIGHT + DEPTH] = ct_ref[...].astype(F32)
    block[4:6, :] = bt_ref[...].astype(F32)
    for peer in range(N_J * N_K):
        sent_ref[peer] = block[...]


def repack_kernel(place, got_ref, sent_ref, rows_b, rows_c):
    jb, kb = place[0], place[2]
    for k in range(N_K):
        rows_b[2 * k : 2 * k + 2, :] = got_ref[jb * N_K + k, 4:6, :]
    for j in range(N_J):
        rows_c[4 * j : 4 * j + 4, :] = got_ref[j * N_K + kb, 0:4, :]
    b, c = rows_b[...].astype(BF16), rows_c[...].astype(BF16)
    for peer in range(N_Z):
        sent_ref[peer, 0:16, :] = b
        sent_ref[peer, 16:32, :] = c


def rows_kernel(got_ref, fa_ref, rows_a):
    for peer in range(N_J * N_K):
        rows_a[4 * peer : 4 * peer + 4, :] = got_ref[peer, 0:4, :]
    fa_ref[...] = rows_a[...].T[0:HEIGHT]


def in_pairs(k, a, c_ref):
    return jnp.concatenate([c_ref[pl.ds(k + s, 1), :] * a for s in range(EACH)], axis=0)


def weight_of(seen_ref, k):
    return seen_ref[pl.ds(k * HEIGHT, ROWS), :].astype(F32)


def add_products(k, weighted, paired, a, b, c_ref, part_a, part_b, part_c):
    part_b[...] += lax.dot_general(weighted, paired, (((0,), (0,)), ((), ())), preferred_element_type=F32)
    mixture = jnp.dot(weighted, b, preferred_element_type=F32)
    total = part_a[...]
    for s in range(EACH):
        slab = mixture[s * HEIGHT : (s + 1) * HEIGHT]
        total = total + slab * c_ref[pl.ds(k + s, 1), :]
        part_c[pl.ds(k + s, 1), :] = jnp.sum(slab * a, axis=0, keepdims=True)
    part_a[...] = total


def hand_out(part_a, part_b, part_c, sent_ref, c_out):
    a, b = part_a[...].astype(BF16), part_b[...].astype(BF16)
    for peer in range(N_K):
        sent_ref[peer, 0:HEIGHT, :] = a
        sent_ref[peer, HEIGHT:AB, :] = b
    c_out[...] = part_c[...]


def first_kernel(got_ref, fa_ref, values_ref, seen_ref, sent_ref, c_out, fb_ref, fbt_ref, fc_ref, part_a, part_b, part_c):
    c = jnp.concatenate([got_ref[z, 16:32, :].astype(F32) for z in range(N_Z)], axis=0)
    fc_ref[...] = c.T[HEIGHT : HEIGHT + DEPTH]
    bt = jnp.concatenate([got_ref[z, 0:16, :] for z in range(N_Z)], axis=0)
    fbt_ref[...] = bt
    fb_ref[...] = bt.astype(F32).T.astype(BF16)
    part_a[...] = jnp.zeros_like(part_a)
    part_b[...] = jnp.zeros_like(part_b)

    @pl.loop(0, DEPTH, step=EACH, unroll=True)
    def _(k):
        a = fa_ref[...]
        paired = in_pairs(k, a, fc_ref).astype(BF16)
        fitted = jnp.dot(paired, fbt_ref[...], preferred_element_type=F32)
        values = values_ref[pl.ds(k * HEIGHT, ROWS), :].astype(F32)
        errors = (values - weight_of(seen_ref, k) * fitted).astype(BF16)
        add_products(k, errors, paired, a, fb_ref[...], fc_ref, part_a, part_b, part_c)

    hand_out(part_a, part_b, part_c, sent_ref, c_out)


def middle_kernel(got_ref, c_ref, sent_ref, a_ref):
    total = got_ref[0].astype(F32)
    for peer in range(1, N_K):
        total = total + got_ref[peer].astype(F32)
    a_ref[...] = total[0:HEIGHT]
    b = total[HEIGHT:AB].astype(BF16)
    c = c_ref[...].astype(BF16)
    for peer in range(N_Z):
        sent_ref[peer, 0:WIDTH, :] = b
        sent_ref[peer, WIDTH:BC, :] = c


def take_totals(got_ref, a_ref, out):
    total = got_ref[0].astype(F32)
    for peer in range(1, N_Z):
        total = total + got_ref[peer].astype(F32)
    out[0:HEIGHT, :] = a_ref[...]
    out[HEIGHT : HEIGHT + BC, :] = total


def tangent_at(k, paired, fa_ref, fc_ref, fbt_ref, hat_a, hat_bt, hat_c):
    sideways = (in_pairs(k, fa_ref[...], hat_c) + in_pairs(k, hat_a[...], fc_ref)).astype(BF16)
    return jnp.dot(paired, hat_bt[...], preferred_element_type=F32) + jnp.dot(
        sideways, fbt_ref[...], preferred_element_type=F32
    )


def round_hats(direction, hat_a, hat_bt, hat_c):
    hat_a[...] = direction[0:HEIGHT].astype(BF16).astype(F32)
    hat_bt[...] = direction[HEIGHT:AB].T.astype(BF16)
    hat_c[...] = direction[AB:].astype(BF16).astype(F32)


def second_kernel(got_ref, a_sum, seen_ref, fa_ref, fb_ref, fbt_ref, fc_ref,
                  sent_ref, c_out, grad_ref, tangent_ref, sum_ref,
                  part_a, part_b, part_c, hat_a, hat_bt, hat_c):
    take_totals(got_ref, a_sum, grad_ref)
    round_hats(grad_ref[...], hat_a, hat_bt, hat_c)
    part_a[...] = jnp.zeros_like(part_a)
    part_b[...] = jnp.zeros_like(part_b)
    sum_ref[...] = jnp.zeros_like(sum_ref)

    @pl.loop(0, DEPTH, step=EACH, unroll=True)
    def _(k):
        a = fa_ref[...]
        paired = in_pairs(k, a, fc_ref).astype(BF16)
        tangent = tangent_at(k, paired, fa_ref, fc_ref, fbt_ref, hat_a, hat_bt, hat_c)
        weighted = weight_of(seen_ref, k) * tangent
        tangent_ref[pl.ds(k * HEIGHT, ROWS), :] = tangent
        sum_ref[...] += jnp.sum((weighted * tangent).reshape(ROWS // 8, 8, WIDTH), axis=0)
        add_products(k, weighted.astype(BF16), paired, a, fb_ref[...], fc_ref, part_a, part_b, part_c)

    hand_out(part_a, part_b, part_c, sent_ref, c_out)


def total_of(x):
    return jnp.sum(jnp.sum(x, axis=0, keepdims=True), axis=1, keepdims=True)


def share_of(x):
    return (
        total_of(x[0:HEIGHT]) * (1.0 / (N_J * N_K))
        + total_of(x[HEIGHT:AB]) * (1.0 / (N_Z * N_K))
        + total_of(x[AB:]) * (1.0 / (N_Z * N_J))
    )


def third_kernel(got_ref, a_sum, seen_ref, fa_ref, fbt_ref, fc_ref, grad_ref, tangent_ref, sum_ref,
                 sent_ref, own_ref, rest_ref, hat_a, hat_bt, hat_c, sum_rest, sum_both):
    take_totals(got_ref, a_sum, rest_ref)
    grad, product = grad_ref[...], rest_ref[...]
    length = share_of(grad * grad)
    level = jnp.where(length > 0.0, share_of(grad * product) / jnp.where(length > 0.0, length, 1.0), 0.0)
    rest = product - level * grad
    rest_ref[...] = rest
    round_hats(rest, hat_a, hat_bt, hat_c)
    sum_rest[...] = jnp.zeros_like(sum_rest)
    sum_both[...] = jnp.zeros_like(sum_both)

    @pl.loop(0, DEPTH, step=EACH, unroll=True)
    def _(k):
        paired = in_pairs(k, fa_ref[...], fc_ref).astype(BF16)
        tangent = tangent_at(k, paired, fa_ref, fc_ref, fbt_ref, hat_a, hat_bt, hat_c)
        weighted = weight_of(seen_ref, k) * tangent
        before = tangent_ref[pl.ds(k * HEIGHT, ROWS), :]
        sum_rest[...] += jnp.sum((weighted * tangent).reshape(ROWS // 8, 8, WIDTH), axis=0)
        sum_both[...] += jnp.sum((weighted * before).reshape(ROWS // 8, 8, WIDTH), axis=0)

    lane = lax.broadcasted_iota(jnp.int32, (1, 128), 1)
    line = jnp.zeros((1, 128), F32)
    for place, value in enumerate(
        (
            level,
            length,
            share_of(grad * rest),
            share_of(rest * rest),
            total_of(sum_ref[...]),
            total_of(sum_both[...]),
            total_of(sum_rest[...]),
        )
    ):
        line = jnp.where(lane == place, value, line)
    own_ref[...] = jnp.broadcast_to(line, (8, 128))
    for peer in range(N_Z * N_J * N_K):
        sent_ref[peer] = line


def columns_kernel(place, grad_ref, rest_ref, out_ref):
    z, jb, kb = place[1], place[0], place[2]
    for at, x in ((0, grad_ref), (16, rest_ref)):
        rows = pltpu.roll(x[0:HEIGHT, :], (128 - (jb * N_K + kb) * 4) % 128, 1).T
        out_ref[at : at + 4, 0:HEIGHT] = rows[0:4]
        rows = pltpu.roll(x[AB:, :], (128 - (z * N_J + jb) * 4) % 128, 1).T
        out_ref[at : at + 4, HEIGHT : HEIGHT + DEPTH] = rows[0:4]
        rows = pltpu.roll(x[HEIGHT:AB, :], (128 - (z * N_K + kb) * 2) % 128, 1).T
        out_ref[at + 8 : at + 10, :] = rows[0:2]


def last_kernel(got_ref, own_ref, columns_ref, a_ref, b_ref, c_ref):
    table = got_ref[:, 0, :].T
    level, gg, gv, vv, s_gg, s_gv, s_vv = (table[i : i + 1] for i in range(7))

    def add(x):
        return jnp.sum(x, axis=1, keepdims=True)

    norm, norm_seen = add(gg), add(s_gg)
    alpha = norm / (norm + norm_seen)
    near = 1.0 - alpha * (1.0 + level)
    rr = add(near * near * gg - 2.0 * alpha * near * gv + alpha * alpha * vv)
    rg = add(near * gg - alpha * gv)
    s_rr = add(near * near * s_gg - 2.0 * alpha * near * s_gv + alpha * alpha * s_vv)
    s_rg = add(near * s_gg - alpha * s_gv)
    beta = rr / norm
    curve = (s_rr + rr) + 2.0 * beta * (s_rg + rg) + beta * beta * (norm_seen + norm)
    step = rr / curve
    own_near = 1.0 - alpha * (1.0 + own_ref[0:1, 0:1])
    x = (alpha + step * (own_near + beta)) * columns_ref[0:16, :] - (step * alpha) * columns_ref[16:32, :]
    a_ref[...] = x[0:4, 0:HEIGHT]
    c_ref[...] = x[0:4, HEIGHT : HEIGHT + DEPTH]
    b_ref[...] = x[8:10, :]


def local(tensor, observed, factor_a, factor_b, factor_c):
    z, jb, kb = lax.axis_index("ia"), lax.axis_index(JA), lax.axis_index(KA)
    place = jnp.stack([jb, z, kb]).astype(jnp.int32)
    weight = (observed.astype(F32) * SCALE).astype(BF16).reshape(CELLS, WIDTH)
    values = tensor.reshape(CELLS, WIDTH) * weight
    tile = lambda rows: ((rows, RANK), F32)
    sums = [tile(HEIGHT), tile(WIDTH), tile(DEPTH)]
    hats = [tile(HEIGHT), ((RANK, WIDTH), BF16), tile(DEPTH)]

    (sent,) = call(
        pack_kernel, [((N_J * N_K, 8, 128), F32)], factor_a.T, factor_b.T, factor_c.T, scratch=[tile(8)]
    )
    shards = exchange(sent, PLANE)
    (sent,) = call(repack_kernel, [((N_Z, 32, 128), BF16)], place, shards, scratch=[tile(16), tile(16)])
    got = exchange(sent, "ia")
    (fa,) = call(rows_kernel, [tile(HEIGHT)], shards, scratch=[tile(128)])

    sent_types = [((N_K, AB, RANK), BF16), tile(DEPTH)]
    sent, part_c, fb, fbt, fc = call(
        first_kernel,
        sent_types + [((WIDTH, RANK), BF16), ((RANK, WIDTH), BF16), tile(DEPTH)],
        got, fa, values, weight, scratch=sums,
    )

    def summed(sent, part_c):
        got = exchange(sent, KA)
        sent, part_a = call(
            middle_kernel, [((N_Z, BC, RANK), BF16), tile(HEIGHT)], got, over_ja(part_c)
        )
        return exchange(sent, "ia"), over_ja(part_a)

    sent, part_c, grad, tangent, sum_gg = call(
        second_kernel,
        sent_types + [tile(AB + DEPTH), tile(CELLS), tile(8)],
        *summed(sent, part_c), weight, fa, fb, fbt, fc, scratch=sums + hats,
    )
    sent, own, rest = call(
        third_kernel,
        [((N_Z * N_J * N_K, 1, 128), F32), tile(8), tile(AB + DEPTH)],
        *summed(sent, part_c), weight, fa, fbt, fc, grad, tangent, sum_gg, scratch=hats + [tile(8), tile(8)],
    )
    (columns,) = call(columns_kernel, [tile(32)], place, grad, rest)
    got = exchange(sent, EVERY)
    steps = call(last_kernel, [((4, HEIGHT), F32), ((2, WIDTH), F32), ((4, DEPTH), F32)], got, own, columns)
    return tuple(x.T for x in steps)


def solution(mesh):
    torus = Mesh(mesh.devices.reshape(N_Z, 2, 2, 4, 2), EVERY)
    return jax.shard_map(
        local,
        mesh=torus,
        in_specs=(P(KA, "ia", JA), P(KA, "ia", JA), P("ia", PLANE), P(JA, IA_KA), P(KA, IA_JA)),
        out_specs=(P("ia", PLANE), P(JA, IA_KA), P(KA, IA_JA)),
        check_vma=False,
    )
```

```python
import jax
import jax.numpy as jnp
from jax import lax
from jax.experimental import pallas as pl
from jax.experimental.pallas import tpu as pltpu
from jax.sharding import Mesh
from jax.sharding import PartitionSpec as P

JA = ("ja_0", "ja_1")
KA = ("ka_0", "ka_1")
PLANE = ("ja_0", "ja_1", "ka_0", "ka_1")
IA_KA = ("ia", "ka_0", "ka_1")
IA_JA = ("ia", "ja_0", "ja_1")
EVERY = ("ia", "ja_0", "ja_1", "ka_0", "ka_1")
F32, BF16 = jnp.float32, jnp.bfloat16
DEPTH, HEIGHT, WIDTH, RANK = 32, 64, 128, 128
CELLS = DEPTH * HEIGHT
N_Z, N_J, N_K = 8, 4, 8
SCALE = 1.0 / 4096.0
AB = HEIGHT + WIDTH
BC = WIDTH + DEPTH


def exchange(blocks, axes):
    return lax.all_to_all(blocks, axes, 0, 0, tiled=True)


def position():
    return (
        lax.axis_index("ia"),
        lax.axis_index("ja_0") * 2 + lax.axis_index("ja_1"),
        lax.axis_index("ka_0") * 2 + lax.axis_index("ka_1"),
    )


def swapped(x, axis):
    return lax.ppermute(x, axis, [(0, 1), (1, 0)])


def over_ja(x):
    x = x + swapped(x, "ja_1")
    return x + swapped(x, "ja_0")


def call(kernel, outs, *operands, scratch=()):
    return pl.pallas_call(
        kernel,
        out_shape=[jax.ShapeDtypeStruct(shape, dtype) for shape, dtype in outs],
        in_specs=[
            pl.BlockSpec(memory_space=pltpu.VMEM)
            for x in operands
        ],
        out_specs=[pl.BlockSpec(memory_space=pltpu.VMEM) for _ in outs],
        scratch_shapes=[pltpu.VMEM(shape, dtype) for shape, dtype in scratch],
        compiler_params=pltpu.CompilerParams(vmem_limit_bytes=48 * 2**20),
    )(*operands)


def pack_kernel(at_ref, bt_ref, ct_ref, sent_ref, block):
    block[...] = jnp.zeros_like(block)
    block[0:4, 0:HEIGHT] = at_ref[...].astype(F32)
    block[0:4, HEIGHT : HEIGHT + DEPTH] = ct_ref[...].astype(F32)
    block[4:6, :] = bt_ref[...].astype(F32)
    for peer in range(N_J * N_K):
        sent_ref[peer] = block[...]


def repack_kernel(got_ref, sent_ref, rows_b, rows_c):
    _, jb, kb = position()
    for k in range(N_K):
        rows_b[2 * k : 2 * k + 2, :] = got_ref[jb * N_K + k, 4:6, :]
    for j in range(N_J):
        rows_c[4 * j : 4 * j + 4, :] = got_ref[j * N_K + kb, 0:4, :]
    b, c = rows_b[...].astype(BF16), rows_c[...].astype(BF16)
    for peer in range(N_Z):
        sent_ref[peer, 0:16, :] = b
        sent_ref[peer, 16:32, :] = c


def rows_kernel(got_ref, fa_ref, rows_a):
    for peer in range(N_J * N_K):
        rows_a[4 * peer : 4 * peer + 4, :] = got_ref[peer, 0:4, :]
    fa_ref[...] = rows_a[...].T[0:HEIGHT]


def in_pairs(k, each, a, c_ref):
    return jnp.concatenate([c_ref[pl.ds(k + s, 1), :] * a for s in range(each)], axis=0)


def weight_of(seen_ref, k, rows):
    return seen_ref[pl.ds(k * HEIGHT, rows), :].astype(F32)


def add_products(k, weighted, paired, a, bt, c_ref, part_a, part_b, part_c):
    part_b[...] += lax.dot_general(paired, weighted, (((0,), (0,)), ((), ())), preferred_element_type=F32)
    mixture = lax.dot_general(weighted, bt, (((1,), (1,)), ((), ())), preferred_element_type=F32)
    total = part_a[...]
    for s in range(weighted.shape[0] // HEIGHT):
        slab = mixture[s * HEIGHT : (s + 1) * HEIGHT]
        total = total + slab * c_ref[pl.ds(k + s, 1), :]
        part_c[pl.ds(k + s, 1), :] = jnp.sum(slab * a, axis=0, keepdims=True)
    part_a[...] = total


def hand_out(part_a, part_b, part_c, sent_ref, c_out):
    a, b = part_a[...].astype(BF16), part_b[...].astype(BF16)
    for peer in range(N_K):
        sent_ref[peer, 0:HEIGHT, :] = a
        sent_ref[peer, HEIGHT:AB, :] = b
    c_out[...] = part_c[...]


def first_kernel(got_ref, fa_ref, values_ref, seen_ref, sent_ref, c_out, fbt_ref, fc_ref, part_a, part_b, part_c):
    c = jnp.concatenate([got_ref[z, 16:32, :].astype(F32) for z in range(N_Z)], axis=0)
    fc_ref[...] = c.T[HEIGHT : HEIGHT + DEPTH]
    bt = jnp.concatenate([got_ref[z, 0:16, :] for z in range(N_Z)], axis=0)
    fbt_ref[...] = bt
    part_a[...] = jnp.zeros_like(part_a)
    part_b[...] = jnp.zeros_like(part_b)

    each = 16
    rows = each * HEIGHT

    @pl.loop(0, DEPTH, step=each, unroll=True)
    def _(k):
        a = fa_ref[...]
        paired = in_pairs(k, each, a, fc_ref).astype(BF16)
        fitted = jnp.dot(paired, fbt_ref[...], preferred_element_type=F32)
        values = values_ref[pl.ds(k * HEIGHT, rows), :].astype(F32)
        errors = (values - weight_of(seen_ref, k, rows) * fitted).astype(BF16)
        add_products(k, errors, paired, a, fbt_ref[...], fc_ref, part_a, part_b, part_c)

    hand_out(part_a, part_b, part_c, sent_ref, c_out)


def middle_kernel(got_ref, c_ref, sent_ref, a_ref):
    total = got_ref[0].astype(F32)
    for peer in range(1, N_K):
        total = total + got_ref[peer].astype(F32)
    a_ref[...] = total[0:HEIGHT]
    b = total[HEIGHT:AB].astype(BF16)
    c = c_ref[...].astype(BF16)
    for peer in range(N_Z):
        sent_ref[peer, 0:WIDTH, :] = b
        sent_ref[peer, WIDTH:BC, :] = c


def take_totals(got_ref, a_ref, out):
    total = got_ref[0].astype(F32)
    for peer in range(1, N_Z):
        total = total + got_ref[peer].astype(F32)
    out[0:HEIGHT, :] = a_ref[...]
    out[HEIGHT : HEIGHT + BC, :] = total


def tangent_at(k, each, paired, fa_ref, fc_ref, fbt_ref, hat_a, hat_bt, hat_c):
    sideways = (in_pairs(k, each, fa_ref[...], hat_c) + in_pairs(k, each, hat_a[...], fc_ref)).astype(BF16)
    return jnp.dot(paired, hat_bt[...], preferred_element_type=F32) + jnp.dot(
        sideways, fbt_ref[...], preferred_element_type=F32
    )


def round_hats(direction, hat_a, hat_bt, hat_c):
    hat_a[...] = direction[0:HEIGHT].astype(BF16).astype(F32)
    hat_bt[...] = direction[HEIGHT:AB].astype(BF16)
    hat_c[...] = direction[AB:].astype(BF16).astype(F32)


def second_kernel(got_ref, a_sum, seen_ref, fa_ref, fbt_ref, fc_ref,
                  sent_ref, c_out, grad_ref, tangent_ref, sum_ref,
                  part_a, part_b, part_c, hat_a, hat_bt, hat_c):
    take_totals(got_ref, a_sum, grad_ref)
    round_hats(grad_ref[...], hat_a, hat_bt, hat_c)
    part_a[...] = jnp.zeros_like(part_a)
    part_b[...] = jnp.zeros_like(part_b)
    sum_ref[...] = jnp.zeros_like(sum_ref)

    each = 8
    rows = each * HEIGHT

    @pl.loop(0, DEPTH, step=each, unroll=True)
    def _(k):
        a = fa_ref[...]
        paired = in_pairs(k, each, a, fc_ref).astype(BF16)
        tangent = tangent_at(k, each, paired, fa_ref, fc_ref, fbt_ref, hat_a, hat_bt, hat_c)
        weighted = weight_of(seen_ref, k, rows) * tangent
        tangent_ref[pl.ds(k * HEIGHT, rows), :] = tangent
        sum_ref[...] += jnp.sum((weighted * tangent).reshape(rows // 8, 8, WIDTH), axis=0)
        add_products(k, weighted.astype(BF16), paired, a, fbt_ref[...], fc_ref, part_a, part_b, part_c)

    hand_out(part_a, part_b, part_c, sent_ref, c_out)


def total_of(x):
    return jnp.sum(jnp.sum(x, axis=0, keepdims=True), axis=1, keepdims=True)


def share_of(x):
    return (
        total_of(x[0:HEIGHT]) * (1.0 / (N_J * N_K))
        + total_of(x[HEIGHT:AB]) * (1.0 / (N_Z * N_K))
        + total_of(x[AB:]) * (1.0 / (N_Z * N_J))
    )


def third_kernel(got_ref, a_sum, seen_ref, fa_ref, fbt_ref, fc_ref, grad_ref, tangent_ref, sum_ref,
                 sent_ref, own_ref, rest_ref, hat_a, hat_bt, hat_c, sum_rest, sum_both):
    take_totals(got_ref, a_sum, rest_ref)
    grad, product = grad_ref[...], rest_ref[...]
    length = share_of(grad * grad)
    level = jnp.where(length > 0.0, share_of(grad * product) / jnp.where(length > 0.0, length, 1.0), 0.0)
    rest = product - level * grad
    rest_ref[...] = rest
    round_hats(rest, hat_a, hat_bt, hat_c)
    sum_rest[...] = jnp.zeros_like(sum_rest)
    sum_both[...] = jnp.zeros_like(sum_both)

    each = 16
    rows = each * HEIGHT

    @pl.loop(0, DEPTH, step=each, unroll=True)
    def _(k):
        paired = in_pairs(k, each, fa_ref[...], fc_ref).astype(BF16)
        tangent = tangent_at(k, each, paired, fa_ref, fc_ref, fbt_ref, hat_a, hat_bt, hat_c)
        weighted = weight_of(seen_ref, k, rows) * tangent
        before = tangent_ref[pl.ds(k * HEIGHT, rows), :]
        sum_rest[...] += jnp.sum((weighted * tangent).reshape(rows // 8, 8, WIDTH), axis=0)
        sum_both[...] += jnp.sum((weighted * before).reshape(rows // 8, 8, WIDTH), axis=0)

    lane = lax.broadcasted_iota(jnp.int32, (1, 128), 1)
    line = jnp.zeros((1, 128), F32)
    for place, value in enumerate(
        (
            level,
            length,
            share_of(grad * rest),
            share_of(rest * rest),
            total_of(sum_ref[...]),
            total_of(sum_both[...]),
            total_of(sum_rest[...]),
        )
    ):
        line = jnp.where(lane == place, value, line)
    own_ref[...] = jnp.broadcast_to(line, (8, 128))
    for peer in range(N_Z * N_J * N_K):
        sent_ref[peer] = line


def columns_kernel(grad_ref, rest_ref, out_ref):
    z, jb, kb = position()
    for at, x in ((0, grad_ref), (16, rest_ref)):
        rows = pltpu.roll(x[0:HEIGHT, :], (128 - (jb * N_K + kb) * 4) % 128, 1).T
        out_ref[at : at + 4, 0:HEIGHT] = rows[0:4]
        rows = pltpu.roll(x[AB:, :], (128 - (z * N_J + jb) * 4) % 128, 1).T
        out_ref[at : at + 4, HEIGHT : HEIGHT + DEPTH] = rows[0:4]
        rows = pltpu.roll(x[HEIGHT:AB, :], (128 - (z * N_K + kb) * 2) % 128, 0)
        out_ref[at + 8 : at + 10, :] = rows[0:2]


def last_kernel(got_ref, own_ref, columns_ref, a_ref, b_ref, c_ref):
    table = got_ref[:, 0, :].T
    level, gg, gv, vv, s_gg, s_gv, s_vv = (table[i : i + 1] for i in range(7))

    def add(x):
        return jnp.sum(x, axis=1, keepdims=True)

    norm, norm_seen = add(gg), add(s_gg)
    alpha = norm / (norm + norm_seen)
    near = 1.0 - alpha * (1.0 + level)
    rr = add(near * near * gg - 2.0 * alpha * near * gv + alpha * alpha * vv)
    rg = add(near * gg - alpha * gv)
    s_rr = add(near * near * s_gg - 2.0 * alpha * near * s_gv + alpha * alpha * s_vv)
    s_rg = add(near * s_gg - alpha * s_gv)
    beta = rr / norm
    curve = (s_rr + rr) + 2.0 * beta * (s_rg + rg) + beta * beta * (norm_seen + norm)
    step = rr / curve
    own_near = 1.0 - alpha * (1.0 + own_ref[0:1, 0:1])
    x = (alpha + step * (own_near + beta)) * columns_ref[0:16, :] - (step * alpha) * columns_ref[16:32, :]
    a_ref[...] = x[0:4, 0:HEIGHT]
    c_ref[...] = x[0:4, HEIGHT : HEIGHT + DEPTH]
    b_ref[...] = x[8:10, :]


def local(tensor, observed, factor_a, factor_b, factor_c):
    weight = (observed.astype(F32) * SCALE).astype(BF16).reshape(CELLS, WIDTH)
    values = tensor.reshape(CELLS, WIDTH) * weight
    tile = lambda rows: ((rows, RANK), F32)
    sums = [tile(HEIGHT), tile(WIDTH), tile(DEPTH)]
    hats = [tile(HEIGHT), ((RANK, WIDTH), BF16), tile(DEPTH)]

    (sent,) = call(
        pack_kernel, [((N_J * N_K, 8, 128), F32)], factor_a.T, factor_b.T, factor_c.T, scratch=[tile(8)]
    )
    shards = exchange(sent, PLANE)
    (sent,) = call(repack_kernel, [((N_Z, 32, 128), BF16)], shards, scratch=[tile(16), tile(16)])
    got = exchange(sent, "ia")
    (fa,) = call(rows_kernel, [tile(HEIGHT)], shards, scratch=[tile(128)])

    sent_types = [((N_K, AB, RANK), BF16), tile(DEPTH)]
    sent, part_c, fbt, fc = call(
        first_kernel,
        sent_types + [((RANK, WIDTH), BF16), tile(DEPTH)],
        got, fa, values, weight, scratch=sums,
    )

    def summed(sent, part_c):
        got = exchange(sent, KA)
        sent, part_a = call(
            middle_kernel, [((N_Z, BC, RANK), BF16), tile(HEIGHT)], got, over_ja(part_c)
        )
        return exchange(sent, "ia"), over_ja(part_a)

    sent, part_c, grad, tangent, sum_gg = call(
        second_kernel,
        sent_types + [tile(AB + DEPTH), tile(CELLS), tile(8)],
        *summed(sent, part_c), weight, fa, fbt, fc, scratch=sums + hats,
    )
    sent, own, rest = call(
        third_kernel,
        [((N_Z * N_J * N_K, 1, 128), F32), tile(8), tile(AB + DEPTH)],
        *summed(sent, part_c), weight, fa, fbt, fc, grad, tangent, sum_gg, scratch=hats + [tile(8), tile(8)],
    )
    (columns,) = call(columns_kernel, [tile(32)], grad, rest)
    got = exchange(sent, EVERY)
    steps = call(last_kernel, [((4, HEIGHT), F32), ((2, WIDTH), F32), ((4, DEPTH), F32)], got, own, columns)
    return tuple(x.T for x in steps)


def solution(mesh):
    torus = Mesh(mesh.devices.reshape(N_Z, 2, 2, 4, 2), EVERY)
    return jax.shard_map(
        local,
        mesh=torus,
        in_specs=(P(KA, "ia", JA), P(KA, "ia", JA), P("ia", PLANE), P(JA, IA_KA), P(KA, IA_JA)),
        out_specs=(P("ia", PLANE), P(JA, IA_KA), P(KA, IA_JA)),
        check_vma=False,
    )
```

```python
import jax
import jax.numpy as jnp
from jax import lax
from jax.experimental import pallas as pl
from jax.experimental.pallas import tpu as pltpu
from jax.sharding import Mesh
from jax.sharding import PartitionSpec as P

JA = ("ja_0", "ja_1")
KA = ("ka_0", "ka_1")
PLANE = ("ja_0", "ja_1", "ka_0", "ka_1")
IA_KA = ("ia", "ka_0", "ka_1")
IA_JA = ("ia", "ja_0", "ja_1")
EVERY = ("ia", "ja_0", "ja_1", "ka_0", "ka_1")
F32, BF16 = jnp.float32, jnp.bfloat16
DEPTH, HEIGHT, WIDTH, RANK = 32, 64, 128, 128
CELLS = DEPTH * HEIGHT
N_Z, N_J, N_K = 8, 4, 8
SCALE = 1.0 / 4096.0
AB = HEIGHT + WIDTH
BC = WIDTH + DEPTH


def exchange(blocks, axes):
    return lax.all_to_all(blocks, axes, 0, 0, tiled=True)


def position():
    return (
        lax.axis_index("ia"),
        lax.axis_index("ja_0") * 2 + lax.axis_index("ja_1"),
        lax.axis_index("ka_0") * 2 + lax.axis_index("ka_1"),
    )


def swapped(x, axis):
    return lax.ppermute(x, axis, [(0, 1), (1, 0)])


def over_ja(x):
    x = x + swapped(x, "ja_1")
    return x + swapped(x, "ja_0")


def call(kernel, outs, *operands, scratch=()):
    return pl.pallas_call(
        kernel,
        out_shape=[jax.ShapeDtypeStruct(shape, dtype) for shape, dtype in outs],
        in_specs=[
            pl.BlockSpec(memory_space=pltpu.VMEM)
            for x in operands
        ],
        out_specs=[pl.BlockSpec(memory_space=pltpu.VMEM) for _ in outs],
        scratch_shapes=[pltpu.VMEM(shape, dtype) for shape, dtype in scratch],
        compiler_params=pltpu.CompilerParams(vmem_limit_bytes=48 * 2**20),
    )(*operands)


def pack_kernel(at_ref, bt_ref, ct_ref, sent_ref, block):
    block[...] = jnp.zeros_like(block)
    block[0:4, 0:HEIGHT] = at_ref[...].astype(F32)
    block[0:4, HEIGHT : HEIGHT + DEPTH] = ct_ref[...].astype(F32)
    block[4:6, :] = bt_ref[...].astype(F32)
    for peer in range(N_J * N_K):
        sent_ref[peer] = block[...].astype(BF16)


def repack_kernel(got_ref, sent_ref, rows_b, rows_c):
    _, jb, kb = position()
    for k in range(N_K):
        rows_b[2 * k : 2 * k + 2, :] = got_ref[jb * N_K + k].astype(F32)[4:6]
    for j in range(N_J):
        rows_c[4 * j : 4 * j + 4, :] = got_ref[j * N_K + kb].astype(F32)[0:4]
    b, c = rows_b[...].astype(BF16), rows_c[...].astype(BF16)
    for peer in range(N_Z):
        sent_ref[peer, 0:16, :] = b
        sent_ref[peer, 16:32, :] = c


def rows_kernel(got_ref, fa_ref, rows_a):
    for peer in range(N_J * N_K):
        rows_a[4 * peer : 4 * peer + 4, :] = got_ref[peer].astype(F32)[0:4]
    fa_ref[...] = rows_a[...].T[0:HEIGHT]


def in_pairs(k, each, a, c_ref):
    return jnp.concatenate([c_ref[pl.ds(k + s, 1), :] * a for s in range(each)], axis=0)


def weight_of(seen_ref, k, rows):
    return seen_ref[pl.ds(k * HEIGHT, rows), :].astype(F32)


def add_products(k, weighted, paired, a, bt, c_ref, part_a, part_b, part_c):
    part_b[...] += lax.dot_general(paired, weighted, (((0,), (0,)), ((), ())), preferred_element_type=F32)
    mixture = lax.dot_general(weighted, bt, (((1,), (1,)), ((), ())), preferred_element_type=F32)
    total = part_a[...]
    for s in range(weighted.shape[0] // HEIGHT):
        slab = mixture[s * HEIGHT : (s + 1) * HEIGHT]
        total = total + slab * c_ref[pl.ds(k + s, 1), :]
        part_c[pl.ds(k + s, 1), :] = jnp.sum(slab * a, axis=0, keepdims=True)
    part_a[...] = total


def hand_out(part_a, part_b, part_c, sent_ref, c_out):
    a, b = part_a[...].astype(BF16), part_b[...].astype(BF16)
    for peer in range(N_K):
        sent_ref[peer, 0:HEIGHT, :] = a
        sent_ref[peer, HEIGHT:AB, :] = b
    c_out[...] = part_c[...]


def first_kernel(got_ref, fa_ref, values_ref, seen_ref, sent_ref, c_out, fbt_ref, fc_ref, part_a, part_b, part_c):
    c = jnp.concatenate([got_ref[z, 16:32, :].astype(F32) for z in range(N_Z)], axis=0)
    fc_ref[...] = c.T[HEIGHT : HEIGHT + DEPTH]
    bt = jnp.concatenate([got_ref[z, 0:16, :] for z in range(N_Z)], axis=0)
    fbt_ref[...] = bt
    part_a[...] = jnp.zeros_like(part_a)
    part_b[...] = jnp.zeros_like(part_b)

    each = 16
    rows = each * HEIGHT

    @pl.loop(0, DEPTH, step=each, unroll=True)
    def _(k):
        a = fa_ref[...]
        paired = in_pairs(k, each, a, fc_ref).astype(BF16)
        fitted = jnp.dot(paired, fbt_ref[...], preferred_element_type=F32)
        values = values_ref[pl.ds(k * HEIGHT, rows), :].astype(F32)
        errors = (values - weight_of(seen_ref, k, rows) * fitted).astype(BF16)
        add_products(k, errors, paired, a, fbt_ref[...], fc_ref, part_a, part_b, part_c)

    hand_out(part_a, part_b, part_c, sent_ref, c_out)


def middle_kernel(got_ref, c_ref, sent_ref, a_ref):
    total = got_ref[0].astype(F32)
    for peer in range(1, N_K):
        total = total + got_ref[peer].astype(F32)
    a_ref[...] = total[0:HEIGHT]
    b = total[HEIGHT:AB].astype(BF16)
    c = c_ref[...].astype(BF16)
    for peer in range(N_Z):
        sent_ref[peer, 0:WIDTH, :] = b
        sent_ref[peer, WIDTH:BC, :] = c


def take_totals(got_ref, a_ref, out):
    total = got_ref[0].astype(F32)
    for peer in range(1, N_Z):
        total = total + got_ref[peer].astype(F32)
    out[0:HEIGHT, :] = a_ref[...]
    out[HEIGHT : HEIGHT + BC, :] = total


def tangent_at(k, each, paired, fa_ref, fc_ref, fbt_ref, hat_a, hat_bt, hat_c):
    sideways = (in_pairs(k, each, fa_ref[...], hat_c) + in_pairs(k, each, hat_a[...], fc_ref)).astype(BF16)
    return jnp.dot(paired, hat_bt[...], preferred_element_type=F32) + jnp.dot(
        sideways, fbt_ref[...], preferred_element_type=F32
    )


def round_hats(direction, hat_a, hat_bt, hat_c):
    hat_a[...] = direction[0:HEIGHT].astype(BF16).astype(F32)
    hat_bt[...] = direction[HEIGHT:AB].astype(BF16)
    hat_c[...] = direction[AB:].astype(BF16).astype(F32)


def second_kernel(got_ref, a_sum, pairs_ref, seen_ref, fa_ref, fbt_ref, fc_ref,
                  sent_ref, c_out, grad_ref, tangent_ref, sum_ref,
                  part_a, part_b, part_c, hat_a, hat_bt, hat_c):
    take_totals(got_ref, a_sum, grad_ref)
    round_hats(grad_ref[...], hat_a, hat_bt, hat_c)
    part_a[...] = jnp.zeros_like(part_a)
    part_b[...] = jnp.zeros_like(part_b)
    sum_ref[...] = jnp.zeros_like(sum_ref)

    each = 8
    rows = each * HEIGHT

    @pl.loop(0, DEPTH, step=each, unroll=True)
    def _(k):
        a = fa_ref[...]
        paired = pairs_ref[pl.ds(k * HEIGHT, rows), :]
        tangent = tangent_at(k, each, paired, fa_ref, fc_ref, fbt_ref, hat_a, hat_bt, hat_c)
        weighted = weight_of(seen_ref, k, rows) * tangent
        tangent_ref[pl.ds(k * HEIGHT, rows), :] = tangent
        sum_ref[...] += jnp.sum((weighted * tangent).reshape(rows // 8, 8, WIDTH), axis=0)
        add_products(k, weighted.astype(BF16), paired, a, fbt_ref[...], fc_ref, part_a, part_b, part_c)

    hand_out(part_a, part_b, part_c, sent_ref, c_out)


def total_of(x):
    return jnp.sum(jnp.sum(x, axis=0, keepdims=True), axis=1, keepdims=True)


def share_of(x):
    return (
        total_of(x[0:HEIGHT]) * (1.0 / (N_J * N_K))
        + total_of(x[HEIGHT:AB]) * (1.0 / (N_Z * N_K))
        + total_of(x[AB:]) * (1.0 / (N_Z * N_J))
    )


def third_kernel(got_ref, a_sum, pairs_ref, seen_ref, fa_ref, fbt_ref, fc_ref, grad_ref, tangent_ref, sum_ref,
                 sent_ref, own_ref, rest_ref, hat_a, hat_bt, hat_c, sum_rest, sum_both):
    take_totals(got_ref, a_sum, rest_ref)
    grad, product = grad_ref[...], rest_ref[...]
    length = share_of(grad * grad)
    level = jnp.where(length > 0.0, share_of(grad * product) / jnp.where(length > 0.0, length, 1.0), 0.0)
    rest = product - level * grad
    rest_ref[...] = rest
    round_hats(rest, hat_a, hat_bt, hat_c)
    sum_rest[...] = jnp.zeros_like(sum_rest)
    sum_both[...] = jnp.zeros_like(sum_both)

    each = 16
    rows = each * HEIGHT

    @pl.loop(0, DEPTH, step=each, unroll=True)
    def _(k):
        paired = pairs_ref[pl.ds(k * HEIGHT, rows), :]
        tangent = tangent_at(k, each, paired, fa_ref, fc_ref, fbt_ref, hat_a, hat_bt, hat_c)
        weighted = weight_of(seen_ref, k, rows) * tangent
        before = tangent_ref[pl.ds(k * HEIGHT, rows), :]
        sum_rest[...] += jnp.sum((weighted * tangent).reshape(rows // 8, 8, WIDTH), axis=0)
        sum_both[...] += jnp.sum((weighted * before).reshape(rows // 8, 8, WIDTH), axis=0)

    lane = lax.broadcasted_iota(jnp.int32, (1, 128), 1)
    line = jnp.zeros((1, 128), F32)
    for place, value in enumerate(
        (
            level,
            length,
            share_of(grad * rest),
            share_of(rest * rest),
            total_of(sum_ref[...]),
            total_of(sum_both[...]),
            total_of(sum_rest[...]),
        )
    ):
        line = jnp.where(lane == place, value, line)
    own_ref[...] = jnp.broadcast_to(line, (8, 128))
    for peer in range(N_Z * N_J * N_K):
        sent_ref[peer] = line


def take_columns(x, out_ref):
    z, jb, kb = position()
    rows = pltpu.roll(x[0:HEIGHT, :], (128 - (jb * N_K + kb) * 4) % 128, 1).T
    out_ref[0:4, 0:HEIGHT] = rows[0:4]
    rows = pltpu.roll(x[AB:, :], (128 - (z * N_J + jb) * 4) % 128, 1).T
    out_ref[0:4, HEIGHT : HEIGHT + DEPTH] = rows[0:4]
    out_ref[8:10, :] = pltpu.roll(x[HEIGHT:AB, :], (128 - (z * N_K + kb) * 2) % 128, 0)[0:2]


def columns_kernel(rest_ref, out_ref):
    take_columns(rest_ref, out_ref)


def add_pairs_kernel(x_ref, y_ref, fa_ref, fc_ref, sum_ref, pairs_ref):
    sum_ref[...] = x_ref[...] + y_ref[...]
    for k in range(0, DEPTH, 8):
        pairs_ref[k * HEIGHT : (k + 8) * HEIGHT, :] = in_pairs(k, 8, fa_ref[...], fc_ref).astype(BF16)


def add_columns_kernel(x_ref, y_ref, grad_ref, sum_ref, out_ref):
    sum_ref[...] = x_ref[...] + y_ref[...]
    take_columns(grad_ref, out_ref)


def last_kernel(got_ref, own_ref, grad_ref, rest_ref, a_ref, b_ref, c_ref):
    table = got_ref[:, 0, :].T
    level, gg, gv, vv, s_gg, s_gv, s_vv = (table[i : i + 1] for i in range(7))

    def add(x):
        return jnp.sum(x, axis=1, keepdims=True)

    norm, norm_seen = add(gg), add(s_gg)
    alpha = norm / (norm + norm_seen)
    near = 1.0 - alpha * (1.0 + level)
    rr = add(near * near * gg - 2.0 * alpha * near * gv + alpha * alpha * vv)
    rg = add(near * gg - alpha * gv)
    s_rr = add(near * near * s_gg - 2.0 * alpha * near * s_gv + alpha * alpha * s_vv)
    s_rg = add(near * s_gg - alpha * s_gv)
    beta = rr / norm
    curve = (s_rr + rr) + 2.0 * beta * (s_rg + rg) + beta * beta * (norm_seen + norm)
    step = rr / curve
    own_near = 1.0 - alpha * (1.0 + own_ref[0:1, 0:1])
    x = (alpha + step * (own_near + beta)) * grad_ref[...] - (step * alpha) * rest_ref[...]
    a_ref[...] = x[0:4, 0:HEIGHT]
    c_ref[...] = x[0:4, HEIGHT : HEIGHT + DEPTH]
    b_ref[...] = x[8:10, :]


def local(tensor, observed, factor_a, factor_b, factor_c):
    weight = (observed.astype(F32) * SCALE).astype(BF16).reshape(CELLS, WIDTH)
    values = tensor.reshape(CELLS, WIDTH) * weight
    tile = lambda rows: ((rows, RANK), F32)
    sums = [tile(HEIGHT), tile(WIDTH), tile(DEPTH)]
    hats = [tile(HEIGHT), ((RANK, WIDTH), BF16), tile(DEPTH)]

    (sent,) = call(
        pack_kernel, [((N_J * N_K, 8, 128), BF16)], factor_a.T, factor_b.T, factor_c.T, scratch=[tile(8)]
    )
    shards = exchange(sent, PLANE)
    (sent,) = call(repack_kernel, [((N_Z, 32, 128), BF16)], shards, scratch=[tile(16), tile(16)])
    got = exchange(sent, "ia")
    (fa,) = call(rows_kernel, [tile(HEIGHT)], shards, scratch=[tile(128)])

    sent_types = [((N_K, AB, RANK), BF16), tile(DEPTH)]
    sent, part_c, fbt, fc = call(
        first_kernel,
        sent_types + [((RANK, WIDTH), BF16), tile(DEPTH)],
        got, fa, values, weight, scratch=sums,
    )

    def summed(sent, part_c, add, extra, *operands):
        got = exchange(sent, KA)
        sent, part_a = call(
            middle_kernel, [((N_Z, BC, RANK), BF16), tile(HEIGHT)], got, over_ja(part_c)
        )
        part_a, made = call(add, [tile(HEIGHT), extra], part_a, swapped(part_a, "ja_1"), *operands)
        return exchange(sent, "ia"), part_a + swapped(part_a, "ja_0"), made

    got, a_sum, pairs = summed(sent, part_c, add_pairs_kernel, ((CELLS, RANK), BF16), fa, fc)
    sent, part_c, grad, tangent, sum_gg = call(
        second_kernel,
        sent_types + [tile(AB + DEPTH), tile(CELLS), tile(8)],
        got, a_sum, pairs, weight, fa, fbt, fc, scratch=sums + hats,
    )
    got, a_sum, columns_g = summed(sent, part_c, add_columns_kernel, tile(16), grad)
    sent, own, rest = call(
        third_kernel,
        [((N_Z * N_J * N_K, 1, 128), F32), tile(8), tile(AB + DEPTH)],
        got, a_sum, pairs, weight, fa, fbt, fc, grad, tangent, sum_gg, scratch=hats + [tile(8), tile(8)],
    )
    (columns_r,) = call(columns_kernel, [tile(16)], rest)
    got = exchange(sent, EVERY)
    steps = call(last_kernel, [((4, HEIGHT), F32), ((2, WIDTH), F32), ((4, DEPTH), F32)], got, own, columns_g, columns_r)
    return tuple(x.T for x in steps)


def solution(mesh):
    torus = Mesh(mesh.devices.reshape(N_Z, 2, 2, 4, 2), EVERY)
    return jax.shard_map(
        local,
        mesh=torus,
        in_specs=(P(KA, "ia", JA), P(KA, "ia", JA), P("ia", PLANE), P(JA, IA_KA), P(KA, IA_JA)),
        out_specs=(P("ia", PLANE), P(JA, IA_KA), P(KA, IA_JA)),
        check_vma=False,
    )
```

```python
import jax
import jax.numpy as jnp
from jax import lax
from jax.experimental import pallas as pl
from jax.experimental.pallas import tpu as pltpu
from jax.sharding import Mesh
from jax.sharding import PartitionSpec as P

JA = ("ja_0", "ja_1")
KA = ("ka_0", "ka_1")
PLANE = ("ja_0", "ja_1", "ka_0", "ka_1")
IA_KA = ("ia", "ka_0", "ka_1")
IA_JA = ("ia", "ja_0", "ja_1")
EVERY = ("ia", "ja_0", "ja_1", "ka_0", "ka_1")
F32, BF16 = jnp.float32, jnp.bfloat16
DEPTH, HEIGHT, WIDTH, RANK = 32, 64, 128, 128
CELLS = DEPTH * HEIGHT
N_Z, N_J, N_K = 8, 4, 8
SCALE = 1.0 / 4096.0
AB = HEIGHT + WIDTH
BC = WIDTH + DEPTH


def exchange(blocks, axes):
    return lax.all_to_all(blocks, axes, 0, 0, tiled=True)


def position():
    return (
        lax.axis_index("ia"),
        lax.axis_index("ja_0") * 2 + lax.axis_index("ja_1"),
        lax.axis_index("ka_0") * 2 + lax.axis_index("ka_1"),
    )


def swapped(x, axis):
    return lax.ppermute(x, axis, [(0, 1), (1, 0)])


def over_ja(x):
    x = x + swapped(x, "ja_1")
    return x + swapped(x, "ja_0")


def call(kernel, outs, *operands, scratch=()):
    return pl.pallas_call(
        kernel,
        out_shape=[jax.ShapeDtypeStruct(shape, dtype) for shape, dtype in outs],
        in_specs=[
            pl.BlockSpec(memory_space=pltpu.VMEM)
            for x in operands
        ],
        out_specs=[pl.BlockSpec(memory_space=pltpu.VMEM) for _ in outs],
        scratch_shapes=[pltpu.VMEM(shape, dtype) for shape, dtype in scratch],
        compiler_params=pltpu.CompilerParams(vmem_limit_bytes=48 * 2**20),
    )(*operands)


def pack_kernel(at_hbm, bt_hbm, ct_hbm, sent_ref, block, at_ref, bt_ref, ct_ref, sems):
    copies = [
        pltpu.make_async_copy(source, target, sems.at[i])
        for i, (source, target) in enumerate(((at_hbm, at_ref), (bt_hbm, bt_ref), (ct_hbm, ct_ref)))
    ]
    for copy in copies:
        copy.start()
    block[...] = jnp.zeros_like(block)
    for copy in copies:
        copy.wait()
    block[0:4, 0:HEIGHT] = at_ref[...].astype(F32)
    block[0:4, HEIGHT : HEIGHT + DEPTH] = ct_ref[...].astype(F32)
    block[4:6, :] = bt_ref[...].astype(F32)
    for peer in range(N_J * N_K):
        sent_ref[peer] = block[...].astype(BF16)


def repack_kernel(got_ref, sent_ref, rows_b, rows_c):
    _, jb, kb = position()
    for k in range(N_K):
        rows_b[2 * k : 2 * k + 2, :] = got_ref[jb * N_K + k].astype(F32)[4:6]
    for j in range(N_J):
        rows_c[4 * j : 4 * j + 4, :] = got_ref[j * N_K + kb].astype(F32)[0:4]
    b, c = rows_b[...].astype(BF16), rows_c[...].astype(BF16)
    for peer in range(N_Z):
        sent_ref[peer, 0:16, :] = b
        sent_ref[peer, 16:32, :] = c


def rows_kernel(got_ref, fa_ref, rows_a):
    for peer in range(N_J * N_K):
        rows_a[4 * peer : 4 * peer + 4, :] = got_ref[peer].astype(F32)[0:4]
    fa_ref[...] = rows_a[...].T[0:HEIGHT]


def in_pairs(k, each, a, c_ref):
    return jnp.concatenate([c_ref[pl.ds(k + s, 1), :] * a for s in range(each)], axis=0)


def weight_of(seen_ref, k, rows):
    return seen_ref[pl.ds(k * HEIGHT, rows), :].astype(F32)


def add_products(k, weighted, paired, a, bt, c_ref, part_a, part_b, part_c):
    part_b[...] += lax.dot_general(paired, weighted, (((0,), (0,)), ((), ())), preferred_element_type=F32)
    mixture = lax.dot_general(weighted, bt, (((1,), (1,)), ((), ())), preferred_element_type=F32)
    total = part_a[...]
    for s in range(weighted.shape[0] // HEIGHT):
        slab = mixture[s * HEIGHT : (s + 1) * HEIGHT]
        total = total + slab * c_ref[pl.ds(k + s, 1), :]
        part_c[pl.ds(k + s, 1), :] = jnp.sum(slab * a, axis=0, keepdims=True)
    part_a[...] = total


def hand_out(part_a, part_b, part_c, sent_ref, c_out):
    a, b = part_a[...].astype(BF16), part_b[...].astype(BF16)
    for peer in range(N_K):
        sent_ref[peer, 0:HEIGHT, :] = a
        sent_ref[peer, HEIGHT:AB, :] = b
    c_out[...] = part_c[...]


def first_kernel(got_ref, fa_ref, values_ref, seen_ref, sent_ref, c_out, fbt_ref, fc_ref, part_a, part_b, part_c):
    c = jnp.concatenate([got_ref[z, 16:32, :].astype(F32) for z in range(N_Z)], axis=0)
    fc_ref[...] = c.T[HEIGHT : HEIGHT + DEPTH]
    bt = jnp.concatenate([got_ref[z, 0:16, :] for z in range(N_Z)], axis=0)
    fbt_ref[...] = bt
    part_a[...] = jnp.zeros_like(part_a)
    part_b[...] = jnp.zeros_like(part_b)

    each = 16
    rows = each * HEIGHT

    @pl.loop(0, DEPTH, step=each, unroll=True)
    def _(k):
        a = fa_ref[...]
        paired = in_pairs(k, each, a, fc_ref).astype(BF16)
        fitted = jnp.dot(paired, fbt_ref[...], preferred_element_type=F32)
        values = values_ref[pl.ds(k * HEIGHT, rows), :].astype(F32)
        errors = (values - weight_of(seen_ref, k, rows) * fitted).astype(BF16)
        add_products(k, errors, paired, a, fbt_ref[...], fc_ref, part_a, part_b, part_c)

    hand_out(part_a, part_b, part_c, sent_ref, c_out)


def middle_kernel(got_ref, c_ref, sent_ref, a_ref):
    total = got_ref[0].astype(F32)
    for peer in range(1, N_K):
        total = total + got_ref[peer].astype(F32)
    a_ref[...] = total[0:HEIGHT]
    b = total[HEIGHT:AB].astype(BF16)
    c = c_ref[...].astype(BF16)
    for peer in range(N_Z):
        sent_ref[peer, 0:WIDTH, :] = b
        sent_ref[peer, WIDTH:BC, :] = c


def take_totals(got_ref, a_ref, out):
    total = got_ref[0].astype(F32)
    for peer in range(1, N_Z):
        total = total + got_ref[peer].astype(F32)
    out[0:HEIGHT, :] = a_ref[...]
    out[HEIGHT : HEIGHT + BC, :] = total


def tangent_at(k, each, paired, fa_ref, fc_ref, fbt_ref, hat_a, hat_bt, hat_c):
    sideways = (in_pairs(k, each, fa_ref[...], hat_c) + in_pairs(k, each, hat_a[...], fc_ref)).astype(BF16)
    return jnp.dot(paired, hat_bt[...], preferred_element_type=F32) + jnp.dot(
        sideways, fbt_ref[...], preferred_element_type=F32
    )


def round_hats(direction, hat_a, hat_bt, hat_c):
    hat_a[...] = direction[0:HEIGHT].astype(BF16).astype(F32)
    hat_bt[...] = direction[HEIGHT:AB].astype(BF16)
    hat_c[...] = direction[AB:].astype(BF16).astype(F32)


def second_kernel(got_ref, a_sum, pairs_ref, seen_ref, fa_ref, fbt_ref, fc_ref,
                  sent_ref, c_out, grad_ref, tangent_ref, sum_ref,
                  part_a, part_b, part_c, hat_a, hat_bt, hat_c):
    take_totals(got_ref, a_sum, grad_ref)
    round_hats(grad_ref[...], hat_a, hat_bt, hat_c)
    part_a[...] = jnp.zeros_like(part_a)
    part_b[...] = jnp.zeros_like(part_b)
    sum_ref[...] = jnp.zeros_like(sum_ref)

    each = 8
    rows = each * HEIGHT

    @pl.loop(0, DEPTH, step=each, unroll=True)
    def _(k):
        a = fa_ref[...]
        paired = pairs_ref[pl.ds(k * HEIGHT, rows), :]
        tangent = tangent_at(k, each, paired, fa_ref, fc_ref, fbt_ref, hat_a, hat_bt, hat_c)
        weighted = weight_of(seen_ref, k, rows) * tangent
        tangent_ref[pl.ds(k * HEIGHT, rows), :] = tangent
        sum_ref[...] += jnp.sum((weighted * tangent).reshape(rows // 8, 8, WIDTH), axis=0)
        add_products(k, weighted.astype(BF16), paired, a, fbt_ref[...], fc_ref, part_a, part_b, part_c)

    hand_out(part_a, part_b, part_c, sent_ref, c_out)


def total_of(x):
    return jnp.sum(jnp.sum(x, axis=0, keepdims=True), axis=1, keepdims=True)


def share_of(x):
    return (
        total_of(x[0:HEIGHT]) * (1.0 / (N_J * N_K))
        + total_of(x[HEIGHT:AB]) * (1.0 / (N_Z * N_K))
        + total_of(x[AB:]) * (1.0 / (N_Z * N_J))
    )


def third_kernel(got_ref, a_sum, pairs_ref, seen_ref, fa_ref, fbt_ref, fc_ref, grad_ref, tangent_ref, sum_ref,
                 sent_ref, own_ref, rest_ref, hat_a, hat_bt, hat_c, sum_rest, sum_both):
    take_totals(got_ref, a_sum, rest_ref)
    grad, product = grad_ref[...], rest_ref[...]
    length = share_of(grad * grad)
    level = jnp.where(length > 0.0, share_of(grad * product) / jnp.where(length > 0.0, length, 1.0), 0.0)
    rest = product - level * grad
    rest_ref[...] = rest
    round_hats(rest, hat_a, hat_bt, hat_c)
    sum_rest[...] = jnp.zeros_like(sum_rest)
    sum_both[...] = jnp.zeros_like(sum_both)

    each = 16
    rows = each * HEIGHT

    @pl.loop(0, DEPTH, step=each, unroll=True)
    def _(k):
        paired = pairs_ref[pl.ds(k * HEIGHT, rows), :]
        tangent = tangent_at(k, each, paired, fa_ref, fc_ref, fbt_ref, hat_a, hat_bt, hat_c)
        weighted = weight_of(seen_ref, k, rows) * tangent
        before = tangent_ref[pl.ds(k * HEIGHT, rows), :]
        sum_rest[...] += jnp.sum((weighted * tangent).reshape(rows // 8, 8, WIDTH), axis=0)
        sum_both[...] += jnp.sum((weighted * before).reshape(rows // 8, 8, WIDTH), axis=0)

    lane = lax.broadcasted_iota(jnp.int32, (1, 128), 1)
    line = jnp.zeros((1, 128), F32)
    for place, value in enumerate(
        (
            level,
            length,
            share_of(grad * rest),
            share_of(rest * rest),
            total_of(sum_ref[...]),
            total_of(sum_both[...]),
            total_of(sum_rest[...]),
        )
    ):
        line = jnp.where(lane == place, value, line)
    own_ref[...] = jnp.broadcast_to(line, (8, 128))
    for peer in range(N_Z * N_J * N_K):
        sent_ref[peer] = line


def take_columns(x, out_ref):
    z, jb, kb = position()
    rows = pltpu.roll(x[0:HEIGHT, :], (128 - (jb * N_K + kb) * 4) % 128, 1).T
    out_ref[0:4, 0:HEIGHT] = rows[0:4]
    rows = pltpu.roll(x[AB:, :], (128 - (z * N_J + jb) * 4) % 128, 1).T
    out_ref[0:4, HEIGHT : HEIGHT + DEPTH] = rows[0:4]
    out_ref[8:10, :] = pltpu.roll(x[HEIGHT:AB, :], (128 - (z * N_K + kb) * 2) % 128, 0)[0:2]


def columns_kernel(rest_ref, out_ref):
    take_columns(rest_ref, out_ref)


def add_pairs_kernel(x_ref, y_ref, fa_ref, fc_ref, sum_ref, pairs_ref):
    sum_ref[...] = x_ref[...] + y_ref[...]
    for k in range(0, DEPTH, 8):
        pairs_ref[k * HEIGHT : (k + 8) * HEIGHT, :] = in_pairs(k, 8, fa_ref[...], fc_ref).astype(BF16)


def add_columns_kernel(x_ref, y_ref, grad_ref, sum_ref, out_ref):
    sum_ref[...] = x_ref[...] + y_ref[...]
    take_columns(grad_ref, out_ref)


def last_kernel(got_ref, own_ref, grad_ref, rest_ref, a_ref, b_ref, c_ref):
    table = got_ref[:, 0, :].T
    level, gg, gv, vv, s_gg, s_gv, s_vv = (table[i : i + 1] for i in range(7))

    def add(x):
        return jnp.sum(x, axis=1, keepdims=True)

    norm, norm_seen = add(gg), add(s_gg)
    alpha = norm / (norm + norm_seen)
    near = 1.0 - alpha * (1.0 + level)
    rr = add(near * near * gg - 2.0 * alpha * near * gv + alpha * alpha * vv)
    rg = add(near * gg - alpha * gv)
    s_rr = add(near * near * s_gg - 2.0 * alpha * near * s_gv + alpha * alpha * s_vv)
    s_rg = add(near * s_gg - alpha * s_gv)
    beta = rr / norm
    curve = (s_rr + rr) + 2.0 * beta * (s_rg + rg) + beta * beta * (norm_seen + norm)
    step = rr / curve
    own_near = 1.0 - alpha * (1.0 + own_ref[0:1, 0:1])
    x = (alpha + step * (own_near + beta)) * grad_ref[...] - (step * alpha) * rest_ref[...]
    a_ref[...] = x[0:4, 0:HEIGHT]
    c_ref[...] = x[0:4, HEIGHT : HEIGHT + DEPTH]
    b_ref[...] = x[8:10, :]


def local(tensor, observed, factor_a, factor_b, factor_c):
    weight = (observed.astype(F32) * SCALE).astype(BF16).reshape(CELLS, WIDTH)
    values = tensor.reshape(CELLS, WIDTH) * weight
    tile = lambda rows: ((rows, RANK), F32)
    sums = [tile(HEIGHT), tile(WIDTH), tile(DEPTH)]
    hats = [tile(HEIGHT), ((RANK, WIDTH), BF16), tile(DEPTH)]

    shards_t = (factor_a.T, factor_b.T, factor_c.T)
    sent = pl.pallas_call(
        pack_kernel,
        out_shape=jax.ShapeDtypeStruct((N_J * N_K, 8, 128), BF16),
        in_specs=[pl.BlockSpec(memory_space=pl.ANY)] * 3,
        out_specs=pl.BlockSpec(memory_space=pltpu.VMEM),
        scratch_shapes=[pltpu.VMEM((8, 128), F32)]
        + [pltpu.VMEM(x.shape, BF16) for x in shards_t]
        + [pltpu.SemaphoreType.DMA((3,))],
    )(*shards_t)
    shards = exchange(sent, PLANE)
    (sent,) = call(repack_kernel, [((N_Z, 32, 128), BF16)], shards, scratch=[tile(16), tile(16)])
    got = exchange(sent, "ia")
    (fa,) = call(rows_kernel, [tile(HEIGHT)], shards, scratch=[tile(128)])

    sent_types = [((N_K, AB, RANK), BF16), tile(DEPTH)]
    sent, part_c, fbt, fc = call(
        first_kernel,
        sent_types + [((RANK, WIDTH), BF16), tile(DEPTH)],
        got, fa, values, weight, scratch=sums,
    )

    def summed(sent, part_c, add, extra, *operands):
        got = exchange(sent, KA)
        sent, part_a = call(
            middle_kernel, [((N_Z, BC, RANK), BF16), tile(HEIGHT)], got, over_ja(part_c)
        )
        part_a, made = call(add, [tile(HEIGHT), extra], part_a, swapped(part_a, "ja_1"), *operands)
        return exchange(sent, "ia"), part_a + swapped(part_a, "ja_0"), made

    got, a_sum, pairs = summed(sent, part_c, add_pairs_kernel, ((CELLS, RANK), BF16), fa, fc)
    sent, part_c, grad, tangent, sum_gg = call(
        second_kernel,
        sent_types + [tile(AB + DEPTH), tile(CELLS), tile(8)],
        got, a_sum, pairs, weight, fa, fbt, fc, scratch=sums + hats,
    )
    got, a_sum, columns_g = summed(sent, part_c, add_columns_kernel, tile(16), grad)
    sent, own, rest = call(
        third_kernel,
        [((N_Z * N_J * N_K, 1, 128), F32), tile(8), tile(AB + DEPTH)],
        got, a_sum, pairs, weight, fa, fbt, fc, grad, tangent, sum_gg, scratch=hats + [tile(8), tile(8)],
    )
    (columns_r,) = call(columns_kernel, [tile(16)], rest)
    got = exchange(sent, EVERY)
    steps = call(last_kernel, [((4, HEIGHT), F32), ((2, WIDTH), F32), ((4, DEPTH), F32)], got, own, columns_g, columns_r)
    return tuple(x.T for x in steps)


def solution(mesh):
    torus = Mesh(mesh.devices.reshape(N_Z, 2, 2, 4, 2), EVERY)
    return jax.shard_map(
        local,
        mesh=torus,
        in_specs=(P(KA, "ia", JA), P(KA, "ia", JA), P("ia", PLANE), P(JA, IA_KA), P(KA, IA_JA)),
        out_specs=(P("ia", PLANE), P(JA, IA_KA), P(KA, IA_JA)),
        check_vma=False,
    )
```
